256 devices in a mesh: ctx: 32 (over z, y), head: 8 (over x, core).
Axes of the slice: x: 4, y: 4, z: 8, core: 2. Of those that a mesh axis runs over, the one named last changes fastest.
Arguments:
- q_latent: bfloat16 [4096, 32768], P('ctx', 'head'), may hold values from -48 to 48
- q_rope: bfloat16 [4096, 4096], P('ctx', 'head'), may hold values from -6 to 6
- out_grad: bfloat16 [4096, 32768], P('ctx', 'head'), may hold values from -6 to 6
- kv_latent: bfloat16 [128, 128, 512], P('ctx'), may hold values from -6 to 6
- key_rope: bfloat16 [128, 64, 128], P('ctx'), may hold values from -6 to 6
- block_lists: int32 [4096, 16], P('ctx'), may hold values from -1 to 127, as said below
- query_pos: int32 [4096], P('ctx'), may hold values from 0 to 16383, as said below
Outputs:
- dq_latent: bfloat16 [4096, 32768], P('ctx', 'head')
- dq_rope: bfloat16 [4096, 4096], P('ctx', 'head')
- dkv_latent: float32 [128, 128, 512], P('ctx', 'head')
- dkey_rope: float32 [128, 64, 128], P('ctx', 'head')
The draws below stay inside these ranges and needn't reach their ends.
Inputs may be any that keep to these rules, and one draw needn't show every extreme that they name: `query_pos`: query i of the queries held by index c of ctx (rows c * 128 to (c + 1) * 128 - 1) stands at a position of that index's own keys, c * 512 to (c + 1) * 512 - 1. `block_lists`: each row names distinct blocks: first the blocks of the same index of ctx, in ascending order from that index's first block up to and including its own query's block, then blocks of earlier indices of ctx only, then -1. Over the 128 rows of one index of ctx, at most 1 distinct block of any one other index is named, and at most 13 distinct blocks of other indices in all; both bounds are reached on every index that has 13 or more earlier indices. Every index of ctx from 1 on names a block of index 0 other than block 0.
All inputs are finite; a program needn't handle non-finite values.
Results may differ from the reference program's by a relative error of at most 0.013.
Values may be sent and summed in bfloat16 or wider, within the bound.
No kernel may reach another device: no remote copies, remote signals or barrier semaphores. Data moves between devices by JAX's collectives and lax.ppermute only.
A program may use at most 128 MiB of HBM per device.

```python
import jax
import jax.numpy as jnp
from jax import lax

D_LAT = 512
D_ROPE = 64
HEADS = 64
BLOCK = 128
TOPB = 16
CAP = 1
Q_DEV = 128
KEYS_DEV = 512
REMOTE = 13
QUERIES = 4096
SEQ = 16384
NBLK = 128


def shared_positions(key):
    ctx_count = QUERIES // Q_DEV
    starts = jnp.arange(ctx_count, dtype=jnp.int32)[:, None] * KEYS_DEV
    offsets = jax.random.randint(jax.random.fold_in(key, 101), (ctx_count, Q_DEV), 0, KEYS_DEV, dtype=jnp.int32)
    return (starts + offsets).reshape(-1)


def special_rows(positions):
    row_ids = jnp.arange(QUERIES, dtype=jnp.int32)
    return (row_ids % 32 == 0) & (positions % BLOCK > 0)


def latent_table(key):
    base = jnp.clip(jax.random.normal(jax.random.fold_in(key, 202), (SEQ, D_LAT), jnp.float32), -5.0, 5.0)
    positions = shared_positions(key)
    special = special_rows(positions)
    prior = jnp.maximum(positions - 1, 0)
    target = prior + jnp.where(special, 0, SEQ)
    updated = base[prior]
    return base.at[target].set(updated, mode='drop')


def draw_query_pos(key, part):
    return shared_positions(key)


def draw_kv_latent(key, part):
    table = latent_table(key)
    return table.reshape(NBLK, BLOCK, D_LAT).astype(jnp.bfloat16)


def draw_q_latent(key, part):
    key = jax.random.fold_in(key, 7)
    drawn = jnp.clip(jax.random.normal(key, (QUERIES, HEADS, D_LAT), jnp.float32), -5.0, 5.0)
    return drawn.reshape(QUERIES, HEADS * D_LAT).astype(jnp.bfloat16)


def draw_block_lists(key, part):
    positions = shared_positions(key)
    key = jax.random.fold_in(key, 11)
    ctx_count = QUERIES // Q_DEV
    blk_count = KEYS_DEV // BLOCK
    peer_count = REMOTE // CAP
    devices = jnp.arange(ctx_count, dtype=jnp.int32)

    def peer_order(sub_key):
        return jax.random.permutation(sub_key, ctx_count)

    def block_order(sub_key):
        return jax.random.permutation(sub_key, blk_count)
    orders = jax.vmap(peer_order)(jax.random.split(jax.random.fold_in(key, 1), ctx_count)).astype(jnp.int32)
    places = jnp.arange(ctx_count, dtype=jnp.int32)[None, :]
    ranked = jnp.where(orders < devices[:, None], places, ctx_count + places)
    ranked = jnp.where((orders == 0) & (devices[:, None] > 0), -1, ranked)
    picks = jnp.argsort(ranked, axis=1, stable=True)[:, :peer_count]
    peers = jnp.take_along_axis(orders, picks, axis=1)
    block_orders = jax.vmap(block_order)(jax.random.split(jax.random.fold_in(key, 2), ctx_count * peer_count)).astype(jnp.int32)
    block_orders = block_orders.reshape(ctx_count, peer_count, blk_count)[:, :, :CAP]
    sink_blocks = jax.random.randint(jax.random.fold_in(key, 4), (ctx_count, 1, CAP), 1, blk_count, dtype=jnp.int32)
    block_orders = jnp.where(peers[:, :, None] == 0, sink_blocks, block_orders)
    candidates = (peers[:, :, None] * blk_count + block_orders).reshape(ctx_count, REMOTE)
    live_count = jnp.minimum(devices, peer_count) * CAP
    shifts = jax.random.randint(jax.random.fold_in(key, 3), (ctx_count,), 0, REMOTE, dtype=jnp.int32)
    owner_dev = positions // KEYS_DEV
    own_block = positions // BLOCK
    first_block = owner_dev * blk_count
    own_count = own_block - first_block + 1
    live = live_count[owner_dev]
    safe_live = jnp.maximum(live, 1)
    row_index = jnp.arange(QUERIES, dtype=jnp.int32) % Q_DEV
    start = (row_index + shifts[owner_dev]) % safe_live
    taken = jnp.minimum(TOPB - own_count, live)
    slots = jnp.arange(TOPB, dtype=jnp.int32)[None, :]
    remote_step = slots - own_count[:, None]
    pick_at = (start[:, None] + jnp.maximum(remote_step, 0)) % safe_live[:, None]
    remote_block = jnp.take_along_axis(candidates[owner_dev], pick_at, axis=1)
    listed = jnp.where(slots < own_count[:, None], first_block[:, None] + slots, jnp.where(remote_step < taken[:, None], remote_block, -1))
    return listed.astype(jnp.int32)


def block_levels(rng, extent, cuts, least, high):
    gain = 1.0
    for axis_at, parts in cuts:
        steps = jax.random.uniform(jax.random.fold_in(jax.random.fold_in(rng, 6), axis_at), (parts,), jnp.float32, least / len(cuts), high / len(cuts))
        gain = gain * jnp.repeat(jnp.exp(steps), extent[axis_at] // parts).reshape((-1,) + (1,) * (len(extent) - 1 - axis_at))
    return gain


def bell_draw(stream_key, extent, scale, reach, cuts=(), kind=jnp.bfloat16):
    array = scale * jax.random.normal(stream_key, extent, jnp.float32)
    if cuts:
        array = array * block_levels(stream_key, extent, cuts, -0.22, 0.18)
    return jnp.clip(array, -reach, reach).astype(kind)


def setup_inputs(seed: int = 0) -> dict:
    keys = jax.random.split(jax.random.key(seed), 8)
    return {
        "q_latent": draw_q_latent(jax.random.fold_in(keys[7], 71), 0),
        "q_rope": bell_draw(keys[1], (QUERIES, HEADS * D_ROPE), 1.0, 6.0, ((0, 32), (1, 8))),
        "out_grad": bell_draw(keys[2], (QUERIES, HEADS * D_LAT), 1.0, 6.0, ((0, 32), (1, 8))),
        "kv_latent": draw_kv_latent(jax.random.fold_in(keys[7], 71), 0),
        "key_rope": bell_draw(keys[4], (NBLK, BLOCK // 2, 2 * D_ROPE), 1.0, 6.0, ((0, 32),)),
        "block_lists": draw_block_lists(jax.random.fold_in(keys[7], 71), 0),
        "query_pos": draw_query_pos(jax.random.fold_in(keys[7], 71), 0),
    }


SCALE_FACTOR = 192.0 ** -0.5
NEG_FILL = -1.0e30


def reference(q_latent, q_rope, out_grad, kv_latent, key_rope, block_lists, query_pos):
    group_rows = 16
    groups = QUERIES // group_rows
    keys_span = TOPB * BLOCK
    lat_all = q_latent.reshape(groups, group_rows, HEADS, D_LAT)
    rope_all = q_rope.reshape(groups, group_rows, HEADS, D_ROPE)
    grad_all = out_grad.reshape(groups, group_rows, HEADS, D_LAT)
    list_all = block_lists.reshape(groups, group_rows, TOPB)
    pos_all = query_pos.reshape(groups, group_rows)
    rope_table = key_rope.reshape(NBLK, BLOCK, D_ROPE)
    offsets = jnp.arange(BLOCK, dtype=jnp.int32)

    def step(carry, items):
        acc_lat, acc_rope = carry
        lat_q, rope_q, grad_q, lists, positions = items
        valid = lists >= 0
        index = jnp.maximum(lists, 0).astype(jnp.int32)
        keys_lat = kv_latent[index].reshape(group_rows, keys_span, D_LAT).astype(jnp.float32)
        keys_rope = rope_table[index].reshape(group_rows, keys_span, D_ROPE).astype(jnp.float32)
        key_pos = (index[:, :, None] * BLOCK + offsets[None, None, :]).reshape(group_rows, keys_span)
        allowed = jnp.repeat(valid, BLOCK, axis=1) & (key_pos <= positions[:, None])
        lat_f = lat_q.astype(jnp.float32)
        rope_f = rope_q.astype(jnp.float32)
        grad_f = grad_q.astype(jnp.float32)
        scores = (jnp.einsum('ghd,gkd->ghk', lat_f, keys_lat) + jnp.einsum('ghd,gkd->ghk', rope_f, keys_rope)) * SCALE_FACTOR
        key_mask = allowed[:, None, :]
        scores = jnp.where(key_mask, scores, NEG_FILL)
        row_top = jnp.max(scores, axis=2, keepdims=True)
        weights = jnp.where(key_mask, jnp.exp(scores - row_top), 0.0)
        attention = weights / jnp.sum(weights, axis=2, keepdims=True)
        attention_low = attention.astype(jnp.bfloat16).astype(jnp.float32)
        dprobs = jnp.einsum('ghd,gkd->ghk', grad_f, keys_lat)
        row_delta = jnp.sum(attention * dprobs, axis=2, keepdims=True)
        dscores = (attention * (dprobs - row_delta)).astype(jnp.bfloat16).astype(jnp.float32)
        dq_lat = (jnp.einsum('ghk,gkd->ghd', dscores, keys_lat) * SCALE_FACTOR).astype(jnp.bfloat16)
        dq_rot = (jnp.einsum('ghk,gkd->ghd', dscores, keys_rope) * SCALE_FACTOR).astype(jnp.bfloat16)
        d_keys_lat = jnp.einsum('ghk,ghd->gkd', dscores, lat_f) * SCALE_FACTOR + jnp.einsum('ghk,ghd->gkd', attention_low, grad_f)
        d_keys_rope = jnp.einsum('ghk,ghd->gkd', dscores, rope_f) * SCALE_FACTOR
        flat_index = index.reshape(-1)
        acc_lat = acc_lat.at[flat_index].add(d_keys_lat.reshape(group_rows * TOPB, BLOCK, D_LAT))
        acc_rope = acc_rope.at[flat_index].add(d_keys_rope.reshape(group_rows * TOPB, BLOCK, D_ROPE))
        return (acc_lat, acc_rope), (dq_lat, dq_rot)

    start = (jnp.zeros((NBLK, BLOCK, D_LAT), jnp.float32), jnp.zeros((NBLK, BLOCK, D_ROPE), jnp.float32))
    (acc_lat, acc_rope), (dq_lat, dq_rot) = lax.scan(step, start, (lat_all, rope_all, grad_all, list_all, pos_all))
    dq_latent = dq_lat.reshape(QUERIES, HEADS * D_LAT)
    dq_rope = dq_rot.reshape(QUERIES, HEADS * D_ROPE)
    return dq_latent, dq_rope, acc_lat, acc_rope.reshape(NBLK, BLOCK // 2, 2 * D_ROPE)
```

```python
import functools

import jax
import jax.numpy as jnp
from jax import lax
from jax.experimental import pallas as pl
from jax.experimental.pallas import tpu as pltpu
from jax.sharding import PartitionSpec as P

SCALE_FACTOR = 192.0 ** (-0.5)
LOG2E = 1.4426950408889634
NEG_FILL = -1e30
BF = jnp.bfloat16
F32 = jnp.float32
LAT = 512
WIDE = 640
SHARE = 16
REMOTE = 13
OWN = 4
FAR_ROWS = REMOTE * SHARE
GROUP = (REMOTE + OWN) * SHARE
GROUPS = 8
KEYS = GROUP * GROUPS
CHIP = 2 * GROUP
HEADS = 8
ROWS = 1024
CH = 256
NCH = ROWS // CH
CUT = 112
VMEM_LIMIT = 56 * 1024 * 1024
NZ, NY, NX = 8, 4, 4


def params():
    return pltpu.CompilerParams(vmem_limit_bytes=VMEM_LIMIT)


def cost(flops, nbytes):
    return pl.CostEstimate(flops=flops, bytes_accessed=nbytes, transcendentals=0)


def vspec():
    return pl.BlockSpec(memory_space=pltpu.VMEM)


def nt_dot(a, b):
    return lax.dot_general(a, b, (((1,), (1,)), ((), ())), preferred_element_type=F32)


def tn_dot(a, b):
    return lax.dot_general(a, b, (((0,), (0,)), ((), ())), preferred_element_type=F32)


def unpack_rope(packed, core):
    row = lax.broadcasted_iota(jnp.int32, (SHARE, SHARE), 0)
    col = lax.broadcasted_iota(jnp.int32, (SHARE, SHARE), 1)
    pick = jnp.where(col == core * 8 + row // 2, 1.0, 0.0).astype(BF)
    wide = jnp.dot(pick, packed, preferred_element_type=F32)
    lane = lax.broadcasted_iota(jnp.int32, (SHARE, 128), 1)
    odd = lax.broadcasted_iota(jnp.int32, (SHARE, 128), 0) % 2 == 1
    both = jnp.where(odd, pltpu.roll(wide, 64, 1), wide)
    return jnp.where(lane < 64, both, 0.0).astype(BF)


def pack_body(me_ref, kv_ref, rope_ref, out_ref):
    core = me_ref[0] % 2
    for b in range(OWN):
        out_ref[b * SHARE:(b + 1) * SHARE, :LAT] = kv_ref[b]
        out_ref[b * SHARE:(b + 1) * SHARE, LAT:] = unpack_rope(rope_ref[b], core)


def pack_call(me, kv, rope):
    return pl.pallas_call(
        pack_body,
        grid_spec=pltpu.PrefetchScalarGridSpec(
            num_scalar_prefetch=1,
            grid=(1,),
            in_specs=[
                pl.BlockSpec((OWN, SHARE, LAT), lambda i, s: (0, s[0], 0)),
                pl.BlockSpec((OWN, SHARE, 128), lambda i, s: (0, s[0] // 2, 0)),
            ],
            out_specs=pl.BlockSpec((OWN * SHARE, WIDE), lambda i, s: (0, 0)),
        ),
        out_shape=jax.ShapeDtypeStruct((OWN * SHARE, WIDE), BF),
        name="pack_share",
    )(me, kv, rope)


def prep_body(me_ref, kv_ref, rope_ref, q_ref, qr_ref, g_ref, far_ref, pos_ref,
              own_out, q_out, g_out, bias_out):
    me = me_ref[0]
    base = me_ref[1]
    lane = lax.broadcasted_iota(jnp.int32, (128, 128), 1)
    for h in range(HEADS):
        q_out[h * 128:(h + 1) * 128, :LAT] = q_ref[:, h * LAT:(h + 1) * LAT]
        g_out[h * 128:(h + 1) * 128, :] = g_ref[:, h * LAT:(h + 1) * LAT]
        pair = qr_ref[:, (h // 2) * 128:(h // 2 + 1) * 128].astype(F32)
        if h % 2:
            pair = pltpu.roll(pair, 64, 1)
        q_out[h * 128:(h + 1) * 128, LAT:] = jnp.where(lane < 64, pair, 0.0).astype(BF)
    pos = pos_ref[...]
    for g in range(GROUPS):
        dx, cr = g // 2, g % 2
        chip = (me // 2 + NX - dx) % NX
        core = (me % 2 + cr) % 2
        share = chip * 2 + core
        for u in range(REMOTE):
            bias_out[g, u * SHARE:(u + 1) * SHARE, :] = jnp.broadcast_to(
                far_ref[u:u + 1, :], (SHARE, 128)
            )
        for b in range(OWN):
            rows = slice(b * SHARE, (b + 1) * SHARE)
            own_out[g, rows, :LAT] = kv_ref[b, pl.ds(pl.multiple_of(share * SHARE, SHARE), SHARE), :]
            own_out[g, rows, LAT:] = unpack_rope(
                rope_ref[b, pl.ds(pl.multiple_of(chip * SHARE, SHARE), SHARE), :], core
            )
            at = base + b * 128 + share * SHARE + lax.broadcasted_iota(jnp.int32, (SHARE, 128), 0)
            bias_out[g, FAR_ROWS + b * SHARE:FAR_ROWS + (b + 1) * SHARE, :] = jnp.where(
                at <= pos, 0.0, NEG_FILL
            )


def prep_call(me, kv, rope, q, qr, g, far, pos):
    return pl.pallas_call(
        prep_body,
        in_specs=[pl.BlockSpec(memory_space=pltpu.SMEM)] + [vspec()] * 7,
        out_specs=[vspec()] * 4,
        out_shape=[
            jax.ShapeDtypeStruct((GROUPS, OWN * SHARE, WIDE), BF),
            jax.ShapeDtypeStruct((ROWS, WIDE), BF),
            jax.ShapeDtypeStruct((ROWS, LAT), BF),
            jax.ShapeDtypeStruct((GROUPS, GROUP, 128), F32),
        ],
        compiler_params=params(),
        cost_estimate=cost(1000, 10_000_000),
        name="prep_operands",
    )(me, kv, rope, q, qr, g, far, pos)


def pick_y_body(want_ref, *refs):
    shards, outs = refs[:NZ], refs[NZ:]
    for dy in range(NY):
        for r in range(NZ):
            w = jnp.maximum(want_ref[dy, r], 0)
            outs[dy][r * SHARE:(r + 1) * SHARE, :] = shards[r][
                pl.ds(pl.multiple_of(w * SHARE, SHARE), SHARE), :
            ]


def pick_y_call(want, shards):
    return pl.pallas_call(
        pick_y_body,
        in_specs=[pl.BlockSpec(memory_space=pltpu.SMEM)] + [vspec()] * NZ,
        out_specs=[vspec()] * NY,
        out_shape=[jax.ShapeDtypeStruct((NZ * SHARE, WIDE), BF)] * NY,
        compiler_params=params(),
        name="pick_for_y_peers",
    )(want, *shards)


def pick_x_body(src_ref, y0, y1, y2, y3, out_ref, stage):
    span = NZ * SHARE
    for dy, ref in enumerate((y0, y1, y2, y3)):
        stage[dy * span:(dy + 1) * span, :] = ref[...]
    for u in range(REMOTE):
        at = pl.multiple_of(src_ref[u] * SHARE, SHARE)
        out_ref[u * SHARE:(u + 1) * SHARE, :] = stage[pl.ds(at, SHARE), :]


def pick_x_call(src, cols):
    return pl.pallas_call(
        pick_x_body,
        in_specs=[pl.BlockSpec(memory_space=pltpu.SMEM)] + [vspec()] * NY,
        out_specs=vspec(),
        out_shape=jax.ShapeDtypeStruct((FAR_ROWS, WIDE), BF),
        scratch_shapes=[pltpu.VMEM((NY * NZ * SHARE, WIDE), BF)],
        compiler_params=params(),
        name="pick_selected",
    )(src, *cols)


def scores_body(x0, x1, x2a, x2b, x3, c0, c1, c2a, c2b, c3, own, q_ref, g_ref, bias_ref,
                k_out, p_out, ds_out, s_scr, e_scr):
    parts = (
        (x0,), (c0,), (x1,), (c1,), (x2a, x2b), (c2a, c2b), (x3,), (c3,),
    )
    for g, refs in enumerate(parts):
        at = g * GROUP
        for ref in refs:
            n = ref.shape[0]
            k_out[at:at + n, :] = ref[...]
            at += n
        k_out[at:at + OWN * SHARE, :] = own[g]

    def chunk(c, carry):
        at = pl.multiple_of(c * CH, CH)
        q = q_ref[pl.ds(at, CH), :]
        g = g_ref[pl.ds(at, CH), :]
        top = jnp.full((1, CH), -jnp.inf, F32)
        for k in range(NX):
            rows = slice(k * CHIP, (k + 1) * CHIP)
            bias = bias_ref[2 * k:2 * k + 2].reshape(CHIP, 128)
            s = nt_dot(k_out[rows, :], q) * (SCALE_FACTOR * LOG2E)
            s = s + jnp.concatenate([bias, bias], axis=1)
            s_scr[rows, :] = s
            top = jnp.maximum(top, jnp.max(s, axis=0, keepdims=True))
        total = jnp.zeros((1, CH), F32)
        delta = jnp.zeros((1, CH), F32)
        for k in range(NX):
            rows = slice(k * CHIP, (k + 1) * CHIP)
            e = nt_dot(k_out[rows, :LAT], g)
            e_scr[rows, :] = e
            w = jnp.exp2(s_scr[rows, :] - top)
            s_scr[rows, :] = w
            total = total + jnp.sum(w, axis=0, keepdims=True)
            delta = delta + jnp.sum(w * e, axis=0, keepdims=True)
        inv = 1.0 / total
        delta = delta * inv
        for k in range(NX):
            rows = slice(k * CHIP, (k + 1) * CHIP)
            p = s_scr[rows, :] * inv
            p_out[c, rows, :] = p.astype(BF)
            ds_out[c, rows, :] = ((e_scr[rows, :] - delta) * (p * SCALE_FACTOR)).astype(BF)
        return carry

    lax.fori_loop(0, NCH, chunk, 0)


def scores_call(xs, cs, own, q, g, bias):
    return pl.pallas_call(
        scores_body,
        in_specs=[vspec()] * 14,
        out_specs=[vspec()] * 3,
        out_shape=[
            jax.ShapeDtypeStruct((KEYS, WIDE), BF),
            jax.ShapeDtypeStruct((NCH, KEYS, CH), BF),
            jax.ShapeDtypeStruct((NCH, KEYS, CH), BF),
        ],
        scratch_shapes=[pltpu.VMEM((KEYS, CH), F32), pltpu.VMEM((KEYS, CH), F32)],
        compiler_params=params(),
        cost_estimate=cost(2 * KEYS * ROWS * 1152, 16_000_000),
        name="scores",
    )(*xs, *cs, own, q, g, bias)


def dkv_body(p_ref, ds_ref, q_ref, g_ref, keep_ref, send_ref):
    for cr, out in enumerate((keep_ref, send_ref)):
        rows = slice(cr * GROUP, (cr + 1) * GROUP)
        ds = jnp.concatenate([ds_ref[c, rows, :] for c in range(NCH)], axis=1)
        p = jnp.concatenate([p_ref[c, rows, :] for c in range(NCH)], axis=1)
        a = jnp.dot(ds, q_ref[...], preferred_element_type=F32)
        b = jnp.dot(p, g_ref[...], preferred_element_type=F32)
        out[:, :LAT] = (a[:, :LAT] + b).astype(out.dtype)
        out[:, LAT:] = a[:, LAT:].astype(out.dtype)


def dkv_call(dx, p, ds, q, g):
    part = pl.BlockSpec((NCH, CHIP, CH), lambda i: (0, dx, 0))
    return pl.pallas_call(
        dkv_body,
        grid=(1,),
        in_specs=[part, part, pl.BlockSpec((ROWS, WIDE), lambda i: (0, 0)),
                  pl.BlockSpec((ROWS, LAT), lambda i: (0, 0))],
        out_specs=[pl.BlockSpec((GROUP, WIDE), lambda i: (0, 0))] * 2,
        out_shape=[
            jax.ShapeDtypeStruct((GROUP, WIDE), F32),
            jax.ShapeDtypeStruct((GROUP, WIDE), BF),
        ],
        compiler_params=params(),
        cost_estimate=cost(2 * CHIP * ROWS * 1152, 5_000_000),
        name=f"dkv_chunk{dx}",
    )(p, ds, q, g)


def dq_body(ds_ref, k_ref, lat_ref, rope_ref):
    res = tn_dot(ds_ref[0], k_ref[...])
    lat_ref[:, :LAT] = res[:128, :LAT].astype(BF)
    lat_ref[:, LAT:] = res[128:, :LAT].astype(BF)
    lane = lax.broadcasted_iota(jnp.int32, (128, 128), 1)
    odd = pltpu.roll(res[128:, LAT:], 64, 1)
    rope_ref[...] = jnp.where(lane < 64, res[:128, LAT:], odd).astype(BF)


def dq_call(ds, keys):
    return pl.pallas_call(
        dq_body,
        grid=(NCH,),
        in_specs=[
            pl.BlockSpec((1, KEYS, CH), lambda i: (i, 0, 0)),
            pl.BlockSpec((KEYS, WIDE), lambda i: (0, 0)),
        ],
        out_specs=[
            pl.BlockSpec((128, 2 * LAT), lambda i: (0, i)),
            pl.BlockSpec((128, 128), lambda i: (0, i)),
        ],
        out_shape=[
            jax.ShapeDtypeStruct((128, HEADS * LAT), BF),
            jax.ShapeDtypeStruct((128, HEADS * 64), BF),
        ],
        compiler_params=params(),
        cost_estimate=cost(2 * KEYS * ROWS * 640, 8_000_000),
        name="dq",
    )(ds, keys)


def slots_body(at_ref, far_ref, *outs):
    for dy in range(NY):
        for r in range(NZ):
            u = pl.multiple_of(at_ref[dy, r] * SHARE, SHARE)
            outs[dy][r * SHARE:(r + 1) * SHARE, :] = far_ref[pl.ds(u, SHARE), :]


def slots_call(at, far):
    return pl.pallas_call(
        slots_body,
        in_specs=[pl.BlockSpec(memory_space=pltpu.SMEM), vspec()],
        out_specs=[vspec()] * NY,
        out_shape=[jax.ShapeDtypeStruct((NZ * SHARE, WIDE), BF)] * NY,
        compiler_params=params(),
        name="slots_for_y_peers",
    )(at, far)


def gather_grad_body(want_ref, y0, y1, y2, y3, *refs):
    outs, acc = refs[:NZ], refs[NZ]
    acc[...] = jnp.zeros_like(acc)
    for dy, ref in enumerate((y0, y1, y2, y3)):
        for r in range(NZ):
            w = want_ref[dy, r]
            at = pl.multiple_of((r * OWN + jnp.maximum(w, 0)) * SHARE, SHARE)
            piece = ref[r * SHARE:(r + 1) * SHARE, :].astype(F32)
            acc[pl.ds(at, SHARE), :] += jnp.where(w >= 0, piece, 0.0)
    span = OWN * SHARE
    for r in range(NZ):
        outs[r][...] = acc[r * span:(r + 1) * span, :].astype(outs[r].dtype)


def gather_grad_call(want, cols):
    span = OWN * SHARE
    return pl.pallas_call(
        gather_grad_body,
        in_specs=[pl.BlockSpec(memory_space=pltpu.SMEM)] + [vspec()] * NY,
        out_specs=[vspec()] * NZ,
        out_shape=[jax.ShapeDtypeStruct((span, WIDE), F32 if r == 0 else BF) for r in range(NZ)],
        scratch_shapes=[pltpu.VMEM((NZ * span, WIDE), F32)],
        compiler_params=params(),
        name="add_y_peers",
    )(want, *cols)


def finish_body(own_ref, z0_ref, up_ref, down_ref, lat_ref, rope_ref, scr):
    total = own_ref[...] + z0_ref[...] + up_ref[...].astype(F32) + down_ref[...].astype(F32)
    for b in range(OWN):
        lat_ref[b] = total[b * SHARE:(b + 1) * SHARE, :LAT]
    scr[...] = total[:, LAT:]
    half = OWN * SHARE // 2
    even = scr[pl.ds(0, half, 2), :]
    odd = scr[pl.ds(1, half, 2), :]
    lane = lax.broadcasted_iota(jnp.int32, (half, 128), 1)
    both = jnp.where(lane < 64, even, pltpu.roll(odd, 64, 1))
    rope_ref[...] = both.reshape(OWN, SHARE // 2, 128)


def finish_call(own, z0, up, down):
    return pl.pallas_call(
        finish_body,
        in_specs=[vspec()] * 4,
        out_specs=[vspec()] * 2,
        out_shape=[
            jax.ShapeDtypeStruct((OWN, SHARE, LAT), F32),
            jax.ShapeDtypeStruct((OWN, SHARE // 2, 128), F32),
        ],
        scratch_shapes=[pltpu.VMEM((OWN * SHARE, 128), F32)],
        compiler_params=params(),
        name="finish",
    )(own, z0, up, down)


def step_z(a, d):
    return lax.ppermute(a, "ctx", [(i, (i + NY * d) % (NZ * NY)) for i in range(NZ * NY)])


def step_y(a, d):
    return lax.ppermute(
        a, "ctx", [(z * NY + y, z * NY + (y + d) % NY) for z in range(NZ) for y in range(NY)]
    )


def step_x(a, d):
    return lax.ppermute(a, "head", [(i, (i + 2 * d) % (2 * NX)) for i in range(2 * NX)])


def swap_core(a):
    return lax.ppermute(a, "head", [(i, i ^ 1) for i in range(2 * NX)])


def local(q_latent, q_rope, out_grad, kv_latent, key_rope, block_lists, query_pos):
    ctx = lax.axis_index("ctx")
    head = lax.axis_index("head")
    my_z, my_y = ctx // NY, ctx % NY
    me = jnp.stack([head, ctx * (OWN * 128)]).astype(jnp.int32)

    shard = [None] * NZ
    shard[0] = pack_call(me, kv_latent, key_rope)
    for s in range(1, 5):
        shard[s] = step_z(shard[s - 1], 1)
        if s < 4:
            shard[NZ - s] = step_z(shard[(NZ - s + 1) % NZ], -1)

    every = jnp.arange(NZ * NY * OWN, dtype=jnp.int32)
    present = jnp.any(block_lists.reshape(-1)[:, None] == every[None, :], axis=0)
    remote = present & (every // OWN != ctx)
    grid = remote.reshape(NZ * NY, OWN)
    want = jnp.max(jnp.where(grid, jnp.arange(OWN, dtype=jnp.int32)[None, :], -1), axis=1)
    rank = jnp.cumsum(remote.astype(jnp.int32)) - 1
    slot_ids = jnp.arange(16, dtype=jnp.int32)
    match = remote[None, :] & (rank[None, :] == slot_ids[:, None])
    remote_ids = jnp.max(jnp.where(match, every[None, :], -1), axis=1)
    owner = jnp.maximum(remote_ids, 0) // OWN
    src = jnp.where(
        remote_ids >= 0, ((my_y - owner % NY) % NY) * NZ + (my_z - owner // NY) % NZ, 0
    ).astype(jnp.int32)
    dys = jnp.arange(NY, dtype=jnp.int32)
    rs = jnp.arange(NZ, dtype=jnp.int32)
    from_ctx = ((my_z - rs[None, :]) % NZ) * NY + (my_y - dys[:, None]) % NY
    hit = (remote_ids[None, None, :] >= 0) & (
        remote_ids[None, None, :] // OWN == from_ctx[:, :, None]
    )
    back_at = jnp.sum(jnp.where(hit, slot_ids[None, None, :], 0), axis=2).astype(jnp.int32)
    wants = jnp.stack([want] + [step_y(want, -d) for d in range(1, NY)])
    my_col = ((my_z - rs) % NZ) * NY + my_y
    want_slots = wants[:, my_col].astype(jnp.int32)
    chosen = jnp.any(block_lists[:, None, :] == remote_ids[None, :, None], axis=2)
    chosen = chosen & (remote_ids >= 0)[None, :]
    far_bias = jnp.where(chosen, 0.0, NEG_FILL).astype(F32).T

    own_keys, q, g, bias = prep_call(
        me, kv_latent, key_rope, q_latent, q_rope, out_grad, far_bias, query_pos.reshape(1, -1)
    )

    cols = pick_y_call(want_slots, shard)
    cols = [cols[0]] + [step_y(cols[d], d) for d in range(1, NY)]
    x0 = pick_x_call(src, cols)
    x1, x3 = step_x(x0, 1), step_x(x0, -1)
    x2a, x2b = step_x(x1[:CUT], 1), step_x(x3[CUT:], -1)
    xs = [x0, x1, x2a, x2b, x3]
    cs = [swap_core(a) for a in xs]

    keys, p, ds = scores_call(xs, cs, own_keys, q, g, bias)

    half = GROUP // 2 + 8
    sums = {}
    for dx in (2, 1, 3, 0):
        keep, send = dkv_call(dx, p, ds, q, g)
        sums[dx] = keep + swap_core(send).astype(F32)
    t2 = sums[2].astype(BF)
    via_down, via_up = step_x(t2[:half], -1), step_x(t2[half:], 1)
    u1 = jnp.concatenate([sums[1][:half] + via_down.astype(F32), sums[1][half:]], axis=0).astype(BF)
    u3 = jnp.concatenate([sums[3][:half], sums[3][half:] + via_up.astype(F32)], axis=0).astype(BF)
    mine = sums[0] + step_x(u1, -1).astype(F32) + step_x(u3, 1).astype(F32)

    dq_latent, dq_rope = dq_call(ds, keys)

    slots = slots_call(back_at, mine[:FAR_ROWS].astype(BF))
    cols = [slots[0]] + [step_y(slots[d], -d) for d in range(1, NY)]
    acc = gather_grad_call(want_slots, cols)
    cut = OWN * SHARE // 2
    down, up = step_z(acc[4][:cut], -1), step_z(acc[4][cut:], 1)
    v3 = jnp.concatenate([(acc[3][:cut].astype(F32) + down.astype(F32)).astype(BF), acc[3][cut:]], axis=0)
    v5 = jnp.concatenate([acc[5][:cut], (acc[5][cut:].astype(F32) + up.astype(F32)).astype(BF)], axis=0)
    down, up = step_z(v3, -1), step_z(v5, 1)
    for r in (2, 1):
        v = (acc[r].astype(F32) + down.astype(F32)).astype(BF)
        w = (acc[NZ - r].astype(F32) + up.astype(F32)).astype(BF)
        down, up = step_z(v, -1), step_z(w, 1)
    dkv_latent, dkey_rope = finish_call(mine[FAR_ROWS:], acc[0], down, up)
    return (dq_latent, dq_rope, dkv_latent, dkey_rope)


def solution(mesh):
    return jax.shard_map(
        local,
        mesh=mesh,
        in_specs=(
            P("ctx", "head"),
            P("ctx", "head"),
            P("ctx", "head"),
            P("ctx", None, None),
            P("ctx", None, None),
            P("ctx", None),
            P("ctx"),
        ),
        out_specs=(
            P("ctx", "head"),
            P("ctx", "head"),
            P("ctx", "head", None),
            P("ctx", "head", None),
        ),
        check_vma=False,
    )
```

```python
import functools

import jax
import jax.numpy as jnp
from jax import lax
from jax.experimental import pallas as pl
from jax.experimental.pallas import tpu as pltpu
from jax.sharding import PartitionSpec as P

SCALE_FACTOR = 192.0 ** (-0.5)
LOG2E = 1.4426950408889634
NEG_FILL = -1e30
BF = jnp.bfloat16
F32 = jnp.float32
LAT = 512
WIDE = 640
SHARE = 16
REMOTE = 13
OWN = 4
FAR_ROWS = REMOTE * SHARE
GROUP = (REMOTE + OWN) * SHARE
GROUPS = 8
KEYS = GROUP * GROUPS
CHIP = 2 * GROUP
HEADS = 8
ROWS = 1024
CH = 256
NCH = ROWS // CH
SPAN = OWN * SHARE
SLOTS = 32
NZ, NY, NX = 8, 4, 4


def params(mib):
    return pltpu.CompilerParams(vmem_limit_bytes=mib * 1024 * 1024)


def after(x, *deps):
    return lax.optimization_barrier((x,) + deps)[0]


def cost(flops, nbytes):
    return pl.CostEstimate(flops=flops, bytes_accessed=nbytes, transcendentals=0)


def vspec():
    return pl.BlockSpec(memory_space=pltpu.VMEM)


def hbm_spec():
    return pl.BlockSpec(memory_space=pltpu.HBM)


def nt_dot(a, b):
    return lax.dot_general(a, b, (((1,), (1,)), ((), ())), preferred_element_type=F32)


def tn_dot(a, b):
    return lax.dot_general(a, b, (((0,), (0,)), ((), ())), preferred_element_type=F32)


def unpack_rope(packed, core):
    row = lax.broadcasted_iota(jnp.int32, (SHARE, SHARE), 0)
    col = lax.broadcasted_iota(jnp.int32, (SHARE, SHARE), 1)
    pick = jnp.where(col == core * 8 + row // 2, 1.0, 0.0).astype(BF)
    wide = jnp.dot(pick, packed, preferred_element_type=F32)
    lane = lax.broadcasted_iota(jnp.int32, (SHARE, 128), 1)
    odd = lax.broadcasted_iota(jnp.int32, (SHARE, 128), 0) % 2 == 1
    both = jnp.where(odd, pltpu.roll(wide, 64, 1), wide)
    return jnp.where(lane < 64, both, 0.0).astype(BF)


def pack_body(kv_ref, rope_ref, out_ref, lat, rope, sems):
    head = lax.axis_index("head")
    wide = kv_ref.at[:, pl.ds(pl.multiple_of(head * SHARE, SHARE), SHARE), :]
    thin = rope_ref.at[:, pl.ds(pl.multiple_of(head // 2 * SHARE, SHARE), SHARE), :]
    copies = (
        pltpu.make_async_copy(wide, lat, sems.at[0]),
        pltpu.make_async_copy(thin, rope, sems.at[1]),
    )
    for copy in copies:
        copy.start()
    for copy in copies:
        copy.wait()
    for b in range(OWN):
        thin_rows = unpack_rope(rope[b], head % 2)
        for z in range(NZ):
            rows = slice(z * SPAN + b * SHARE, z * SPAN + (b + 1) * SHARE)
            out_ref[rows, :LAT] = lat[b]
            out_ref[rows, LAT:] = thin_rows


def pack_call(kv, rope):
    return pl.pallas_call(
        pack_body,
        in_specs=[hbm_spec()] * 2,
        out_specs=vspec(),
        out_shape=jax.ShapeDtypeStruct((NZ * SPAN, WIDE), BF),
        scratch_shapes=[
            pltpu.VMEM((OWN, SHARE, LAT), BF),
            pltpu.VMEM((OWN, SHARE, 128), BF),
            pltpu.SemaphoreType.DMA((2,)),
        ],
        compiler_params=params(56),
        name="pack_share",
    )(kv, rope)


def share_of(me, g):
    return (me // 2 + NX - g // 2) % NX, (me % 2 + g % 2) % 2


def prep_body(kv_hbm, rope_hbm, q_hbm, qr_hbm, g_hbm, own_out, q_out, g_out,
              kv_ref, rope_ref, qr_ref, sems):
    copies = [
        pltpu.make_async_copy(qr_hbm, qr_ref, sems.at[0]),
        pltpu.make_async_copy(rope_hbm, rope_ref, sems.at[1]),
        pltpu.make_async_copy(kv_hbm, kv_ref, sems.at[2]),
    ]
    for h in range(HEADS):
        cols, rows = pl.ds(h * LAT, LAT), pl.ds(h * 128, 128)
        copies.append(pltpu.make_async_copy(
            q_hbm.at[:, cols], q_out.at[rows, pl.ds(0, LAT)], sems.at[3 + 2 * h]))
        copies.append(pltpu.make_async_copy(
            g_hbm.at[:, cols], g_out.at[rows, :], sems.at[4 + 2 * h]))
    for copy in copies:
        copy.start()
    me = lax.axis_index("head")
    lane = lax.broadcasted_iota(jnp.int32, (128, 128), 1)
    copies[0].wait()
    for h in range(HEADS):
        pair = qr_ref[:, (h // 2) * 128:(h // 2 + 1) * 128].astype(F32)
        if h % 2:
            pair = pltpu.roll(pair, 64, 1)
        q_out[h * 128:(h + 1) * 128, LAT:] = jnp.where(lane < 64, pair, 0.0).astype(BF)
    copies[1].wait()
    for g in range(GROUPS):
        chip, core = share_of(me, g)
        for b in range(OWN):
            own_out[g, b * SHARE:(b + 1) * SHARE, LAT:] = unpack_rope(
                rope_ref[b, pl.ds(pl.multiple_of(chip * SHARE, SHARE), SHARE), :], core
            )
    copies[2].wait()
    for g in range(GROUPS):
        chip, core = share_of(me, g)
        at = pl.multiple_of((chip * 2 + core) * SHARE, SHARE)
        for b in range(OWN):
            own_out[g, b * SHARE:(b + 1) * SHARE, :LAT] = kv_ref[b, pl.ds(at, SHARE), :]
    for copy in copies[3:]:
        copy.wait()


def prep_call(kv, rope, q, qr, g):
    return pl.pallas_call(
        prep_body,
        in_specs=[hbm_spec()] * 5,
        out_specs=[vspec()] * 3,
        out_shape=[
            jax.ShapeDtypeStruct((GROUPS, SPAN, WIDE), BF),
            jax.ShapeDtypeStruct((ROWS, WIDE), BF),
            jax.ShapeDtypeStruct((ROWS, LAT), BF),
        ],
        scratch_shapes=[
            pltpu.VMEM(kv.shape, BF),
            pltpu.VMEM(rope.shape, BF),
            pltpu.VMEM(qr.shape, BF),
            pltpu.SemaphoreType.DMA((3 + 2 * HEADS,)),
        ],
        compiler_params=params(10),
        cost_estimate=cost(1000, 10_000_000),
        name="prep_operands",
    )(kv, rope, q, qr, g)


def pick_y_body(*refs):
    wants, shards, outs = refs[:NY], refs[NY], refs[NY + 1:]
    ctx = lax.axis_index("ctx")
    for r in range(NZ):
        z = (ctx // NY + NZ - r) % NZ
        for dy in range(NY):
            w = jnp.maximum(wants[dy][z * NY + ctx % NY], 0)
            at = pl.multiple_of((z * OWN + w) * SHARE, SHARE)
            outs[dy][r * SHARE:(r + 1) * SHARE, :] = shards[pl.ds(at, SHARE), :]


def pick_y_call(wants, shards):
    return pl.pallas_call(
        pick_y_body,
        in_specs=[pl.BlockSpec(memory_space=pltpu.SMEM)] * NY + [vspec()],
        out_specs=[vspec()] * NY,
        out_shape=[jax.ShapeDtypeStruct((NZ * SHARE, WIDE), BF)] * NY,
        compiler_params=params(4),
        name="pick_for_y_peers",
    )(*wants, shards)


def pick_x_body(src_ref, y0, y1, y2, y3, out_ref, stage):
    span = NZ * SHARE
    for dy, ref in enumerate((y0, y1, y2, y3)):
        stage[dy * span:(dy + 1) * span, :] = ref[...]
    for u in range(REMOTE):
        at = pl.multiple_of(src_ref[u] * SHARE, SHARE)
        out_ref[u * SHARE:(u + 1) * SHARE, :] = stage[pl.ds(at, SHARE), :]


def pick_x_call(src, cols):
    return pl.pallas_call(
        pick_x_body,
        in_specs=[pl.BlockSpec(memory_space=pltpu.SMEM)] + [vspec()] * NY,
        out_specs=vspec(),
        out_shape=jax.ShapeDtypeStruct((FAR_ROWS, WIDE), BF),
        scratch_shapes=[pltpu.VMEM((NY * NZ * SHARE, WIDE), BF)],
        compiler_params=params(4),
        name="pick_selected",
    )(src, *cols)


def scores_body(me_ref, far_ref, pos_ref, x0, x1, x2, x3, c0, c1, c2, c3, own, q_ref, g_ref,
                k_out, p_out, ds_out, s_scr, e_scr, bias_scr):
    me = me_ref[0]
    pos = pos_ref[...] - me_ref[1]
    for u in range(REMOTE):
        line = jnp.broadcast_to(far_ref[u:u + 1, :], (SHARE, 128))
        for g in range(GROUPS):
            bias_scr[g * GROUP + u * SHARE:g * GROUP + (u + 1) * SHARE, :] = line
    step = lax.broadcasted_iota(jnp.int32, (SHARE, 128), 0)
    for g in range(GROUPS):
        chip, core = share_of(me, g)
        for b in range(OWN):
            at = g * GROUP + FAR_ROWS + b * SHARE
            key = step + (b * 128 + (chip * 2 + core) * SHARE)
            bias_scr[at:at + SHARE, :] = jnp.where(key <= pos, 0.0, NEG_FILL)
    for g, ref in enumerate((x0, c0, x1, c1, x2, c2, x3, c3)):
        k_out[g * GROUP:g * GROUP + FAR_ROWS, :] = ref[...]
        k_out[g * GROUP + FAR_ROWS:(g + 1) * GROUP, :] = own[g]

    def chunk(c, carry):
        at = c * CH
        q = q_ref[pl.ds(at, CH), :]
        g = g_ref[pl.ds(at, CH), :]
        top = jnp.full((1, CH), -jnp.inf, F32)
        for k in range(GROUPS):
            rows = slice(k * GROUP, (k + 1) * GROUP)
            bias = bias_scr[rows, :]
            s = nt_dot(k_out[rows, :], q) * (SCALE_FACTOR * LOG2E)
            s = s + jnp.concatenate([bias, bias], axis=1)
            s_scr[rows, :] = s
            top = jnp.maximum(top, jnp.max(s, axis=0, keepdims=True))
        total = jnp.zeros((1, CH), F32)
        delta = jnp.zeros((1, CH), F32)
        for k in range(GROUPS):
            rows = slice(k * GROUP, (k + 1) * GROUP)
            e = nt_dot(k_out[rows, :LAT], g)
            e_scr[rows, :] = e
            w = jnp.exp2(s_scr[rows, :] - top)
            s_scr[rows, :] = w
            total = total + jnp.sum(w, axis=0, keepdims=True)
            delta = delta + jnp.sum(w * e, axis=0, keepdims=True)
        inv = 1.0 / total
        delta = delta * inv
        for k in range(GROUPS):
            rows = slice(k * GROUP, (k + 1) * GROUP)
            p = s_scr[rows, :] * inv
            p_out[c, rows, :] = p.astype(BF)
            ds_out[c, rows, :] = ((e_scr[rows, :] - delta) * (p * SCALE_FACTOR)).astype(BF)
        return carry

    for c in range(NCH):
        chunk(c, 0)


def scores_call(me, far, pos, xs, cs, own, q, g):
    return pl.pallas_call(
        scores_body,
        in_specs=[pl.BlockSpec(memory_space=pltpu.SMEM)] + [vspec()] * 13,
        out_specs=[vspec()] * 3,
        out_shape=[
            jax.ShapeDtypeStruct((KEYS, WIDE), BF),
            jax.ShapeDtypeStruct((NCH, KEYS, CH), BF),
            jax.ShapeDtypeStruct((NCH, KEYS, CH), BF),
        ],
        scratch_shapes=[
            pltpu.VMEM((KEYS, CH), F32),
            pltpu.VMEM((KEYS, CH), F32),
            pltpu.VMEM((KEYS, 128), F32),
        ],
        compiler_params=params(30),
        cost_estimate=cost(2 * KEYS * ROWS * 1152, 16_000_000),
        name="scores",
    )(me, far, pos, *xs, *cs, own, q, g)


def dkv_body(p_ref, ds_ref, q_ref, g_ref, keep_ref, send_ref):
    for cr, out in enumerate((keep_ref, send_ref)):
        rows = slice(cr * GROUP, (cr + 1) * GROUP)
        ds = jnp.concatenate([ds_ref[c, rows, :] for c in range(NCH)], axis=1)
        p = jnp.concatenate([p_ref[c, rows, :] for c in range(NCH)], axis=1)
        a = jnp.dot(ds, q_ref[...], preferred_element_type=F32)
        b = jnp.dot(p, g_ref[...], preferred_element_type=F32)
        out[:, :LAT] = (a[:, :LAT] + b).astype(out.dtype)
        out[:, LAT:] = a[:, LAT:].astype(out.dtype)


def dkv_call(dx, p, ds, q, g):
    part = pl.BlockSpec((NCH, CHIP, CH), lambda i: (0, dx, 0))
    return pl.pallas_call(
        dkv_body,
        grid=(1,),
        in_specs=[part, part, pl.BlockSpec((ROWS, WIDE), lambda i: (0, 0)),
                  pl.BlockSpec((ROWS, LAT), lambda i: (0, 0))],
        out_specs=[pl.BlockSpec((GROUP, WIDE), lambda i: (0, 0))] * 2,
        out_shape=[
            jax.ShapeDtypeStruct((GROUP, WIDE), F32),
            jax.ShapeDtypeStruct((GROUP, WIDE), BF),
        ],
        compiler_params=params(16),
        cost_estimate=cost(2 * CHIP * ROWS * 1152, 5_000_000),
        name=f"dkv_chunk{dx}",
    )(p, ds, q, g)


def dq_body(ds_ref, k_ref, lat_ref, rope_ref):
    res = tn_dot(ds_ref[0], k_ref[...])
    lat_ref[:, :LAT] = res[:128, :LAT].astype(BF)
    lat_ref[:, LAT:] = res[128:, :LAT].astype(BF)
    lane = lax.broadcasted_iota(jnp.int32, (128, 128), 1)
    odd = pltpu.roll(res[128:, LAT:], 64, 1)
    rope_ref[...] = jnp.where(lane < 64, res[:128, LAT:], odd).astype(BF)


def dq_call(ds, keys):
    return pl.pallas_call(
        dq_body,
        grid=(NCH,),
        in_specs=[
            pl.BlockSpec((1, KEYS, CH), lambda i: (i, 0, 0)),
            pl.BlockSpec((KEYS, WIDE), lambda i: (0, 0)),
        ],
        out_specs=[
            pl.BlockSpec((128, 2 * LAT), lambda i: (0, i)),
            pl.BlockSpec((128, 128), lambda i: (0, i)),
        ],
        out_shape=[
            jax.ShapeDtypeStruct((128, HEADS * LAT), BF),
            jax.ShapeDtypeStruct((128, HEADS * 64), BF),
        ],
        compiler_params=params(14),
        cost_estimate=cost(2 * KEYS * ROWS * 640, 8_000_000),
        name="dq",
    )(ds, keys)


def slots_body(at_ref, want_ref, keep_ref, swap_ref, r1_ref, r2_ref, r3_ref,
               slot_out, own_out, far):
    total = keep_ref[...] + swap_ref[...].astype(F32)
    for ref in (r1_ref, r2_ref, r3_ref):
        total = total + ref[...].astype(F32)
    own_out[...] = total[FAR_ROWS:, :]
    far[...] = total[:FAR_ROWS, :]
    lane = lax.broadcasted_iota(jnp.int32, (SHARE, 128), 1)
    for c in range(SLOTS):
        rows = slice(c * SHARE, (c + 1) * SHARE)
        w = want_ref[c]
        flag = jnp.where(w >= 0, 64 + w, 128)
        piece = far[pl.ds(pl.multiple_of(at_ref[c] * SHARE, SHARE), SHARE), :]
        slot_out[rows, :LAT] = piece[:, :LAT].astype(BF)
        slot_out[rows, LAT:] = jnp.where(lane == flag, 1.0, piece[:, LAT:]).astype(BF)


def slots_call(at, want, keep, swap, r1, r2, r3):
    smem = pl.BlockSpec(memory_space=pltpu.SMEM)
    return pl.pallas_call(
        slots_body,
        in_specs=[smem, smem] + [vspec()] * 5,
        out_specs=[vspec()] * 2,
        out_shape=[
            jax.ShapeDtypeStruct((SLOTS * SHARE, WIDE), BF),
            jax.ShapeDtypeStruct((SPAN, WIDE), F32),
        ],
        scratch_shapes=[pltpu.VMEM((FAR_ROWS, WIDE), F32)],
        compiler_params=params(8),
        name="fill_slots",
    )(at, want, keep, swap, r1, r2, r3)


def finish_body(own_ref, back_ref, lat_ref, rope_ref, acc, scr):
    acc[...] = own_ref[...]
    for c in range(SLOTS):
        piece = back_ref[c * SHARE:(c + 1) * SHARE, :].astype(F32)
        for b in range(OWN):
            mine = piece[:, LAT + 64 + b:LAT + 65 + b] > 0.5
            acc[b * SHARE:(b + 1) * SHARE, :] += jnp.where(mine, piece, 0.0)
    for b in range(OWN):
        lat_ref[b] = acc[b * SHARE:(b + 1) * SHARE, :LAT]
    scr[...] = acc[:, LAT:]
    half = SPAN // 2
    even = scr[pl.ds(0, half, 2), :]
    odd = scr[pl.ds(1, half, 2), :]
    lane = lax.broadcasted_iota(jnp.int32, (half, 128), 1)
    both = jnp.where(lane < 64, even, pltpu.roll(odd, 64, 1))
    rope_ref[...] = both.reshape(OWN, SHARE // 2, 128)


def finish_call(own, back):
    return pl.pallas_call(
        finish_body,
        in_specs=[vspec()] * 2,
        out_specs=[vspec()] * 2,
        out_shape=[
            jax.ShapeDtypeStruct((OWN, SHARE, LAT), F32),
            jax.ShapeDtypeStruct((OWN, SHARE // 2, 128), F32),
        ],
        scratch_shapes=[pltpu.VMEM((SPAN, WIDE), F32), pltpu.VMEM((SPAN, 128), F32)],
        compiler_params=params(8),
        name="finish",
    )(own, back)


def step_z(a, d):
    return lax.ppermute(a, "ctx", [(i, (i + NY * d) % (NZ * NY)) for i in range(NZ * NY)])


def step_y(a, d):
    return lax.ppermute(
        a, "ctx", [(z * NY + y, z * NY + (y + d) % NY) for z in range(NZ) for y in range(NY)]
    )


def step_x(a, d):
    return lax.ppermute(a, "head", [(i, (i + 2 * d) % (2 * NX)) for i in range(2 * NX)])


def swap_core(a):
    return lax.ppermute(a, "head", [(i, i ^ 1) for i in range(2 * NX)])


def local(q_latent, q_rope, out_grad, kv_latent, key_rope, block_lists, query_pos):
    ctx = lax.axis_index("ctx")
    head = lax.axis_index("head")
    my_z, my_y = ctx // NY, ctx % NY
    me = jnp.stack([head, ctx * (OWN * 128)]).astype(jnp.int32)

    shard = pack_call(kv_latent, key_rope)
    columns = [[z * NY + y for z in range(NZ)] for y in range(NY)]
    shards = lax.all_to_all(shard, "ctx", 0, 0, tiled=True, axis_index_groups=columns)

    block_lists, me, query_pos = after((block_lists, me, query_pos), shard)
    every = jnp.arange(NZ * NY * OWN, dtype=jnp.int32)
    present = jnp.any(block_lists.reshape(-1)[:, None] == every[None, :], axis=0)
    remote = present & (every // OWN != ctx)
    grid = remote.reshape(NZ * NY, OWN)
    want = jnp.max(jnp.where(grid, jnp.arange(OWN, dtype=jnp.int32)[None, :], -1), axis=1)
    rank = jnp.cumsum(remote.astype(jnp.int32)) - 1
    slot_ids = jnp.arange(16, dtype=jnp.int32)
    match = remote[None, :] & (rank[None, :] == slot_ids[:, None])
    remote_ids = jnp.max(jnp.where(match, every[None, :], -1), axis=1)
    owner = jnp.maximum(remote_ids, 0) // OWN
    src = jnp.where(
        remote_ids >= 0, ((my_y - owner % NY) % NY) * NZ + (my_z - owner // NY) % NZ, 0
    ).astype(jnp.int32)
    ctxs = jnp.arange(SLOTS, dtype=jnp.int32)
    hit = (remote_ids[None, :] >= 0) & (remote_ids[None, :] // OWN == ctxs[:, None])
    back_at = jnp.sum(jnp.where(hit, slot_ids[None, :], 0), axis=1).astype(jnp.int32)
    wants = [want] + [step_y(want, -d) for d in range(1, NY)]
    chosen = jnp.any(block_lists[:, None, :] == remote_ids[None, :, None], axis=2)
    chosen = chosen & (remote_ids >= 0)[None, :]
    far_bias = jnp.where(chosen, 0.0, NEG_FILL).astype(F32).T

    cols = pick_y_call(wants, shards)
    cols = [cols[0]] + [step_y(cols[d], d) for d in range(1, NY)]
    x0 = pick_x_call(src, cols)
    x2, x1, x3 = step_x(x0, 2), step_x(x0, 1), step_x(x0, -1)
    xs = [x0, x1, x2, x3]
    arrays = after((kv_latent, key_rope, q_latent, q_rope, out_grad), x0)
    own_keys, q, g = prep_call(*arrays)
    cs = [swap_core(x0)] + [swap_core(after(a, own_keys)) for a in xs[1:]]

    keys, p, ds = scores_call(me, far_bias, query_pos.reshape(1, -1), xs, cs, own_keys, q, g)

    order = (2, 1, 3, 0)
    keep, send, part, got = {}, {}, {}, {}
    for n, dx in enumerate(order):
        keep[dx], send[dx] = dkv_call(dx, p, ds, q, g)
        p, ds = after((p, ds), send[dx])
        if n:
            prev = order[n - 1]
            part[prev] = (keep[prev] + swap_core(send[prev]).astype(F32)).astype(BF)
            got[prev] = step_x(part[prev], -prev)
            p, ds = after((p, ds), part[prev])
    swap = swap_core(send[0])
    dq_latent, dq_rope = dq_call(ds, keys)
    mine, dq_latent, dq_rope = lax.optimization_barrier((keep[0], dq_latent, dq_rope))

    slots, own = slots_call(back_at, want, mine, swap, got[1], got[2], got[3])
    back = lax.all_to_all(slots, "ctx", split_axis=0, concat_axis=0, tiled=True)
    dkv_latent, dkey_rope = finish_call(own, back)
    return (dq_latent, dq_rope, dkv_latent, dkey_rope)


def solution(mesh):
    return jax.shard_map(
        local,
        mesh=mesh,
        in_specs=(
            P("ctx", "head"),
            P("ctx", "head"),
            P("ctx", "head"),
            P("ctx", None, None),
            P("ctx", None, None),
            P("ctx", None),
            P("ctx"),
        ),
        out_specs=(
            P("ctx", "head"),
            P("ctx", "head"),
            P("ctx", "head", None),
            P("ctx", "head", None),
        ),
        check_vma=False,
    )
```

```python
import functools

import jax
import jax.numpy as jnp
from jax import lax
from jax.experimental import pallas as pl
from jax.experimental.pallas import tpu as pltpu
from jax.sharding import PartitionSpec as P

SCALE_FACTOR = 192.0 ** (-0.5)
LOG2E = 1.4426950408889634
NEG_FILL = -1e30
BF = jnp.bfloat16
F32 = jnp.float32
LAT = 512
WIDE = 640
SHARE = 16
REMOTE = 13
OWN = 4
FAR_ROWS = REMOTE * SHARE
GROUP = (REMOTE + OWN) * SHARE
GROUPS = 8
KEYS = GROUP * GROUPS
CHIP = 2 * GROUP
HEADS = 8
ROWS = 1024
CH = 256
NCH = ROWS // CH
SPAN = OWN * SHARE
SLOTS = 32
TILES = LAT // 128
BLOCK_ROWS = TILES * SHARE
SHARD_ROWS = OWN * BLOCK_ROWS + OWN // 2 * SHARE
COL_LAT = 8 * BLOCK_ROWS
COL_ROWS = COL_LAT + 4 * SHARE
FAR_LAT = REMOTE * BLOCK_ROWS
FAR_PACKED = FAR_LAT + (REMOTE + 1) // 2 * SHARE
GRAD_LAT = (REMOTE + OWN) * BLOCK_ROWS
GRAD_ROWS = GRAD_LAT + (REMOTE + OWN + 1) // 2 * SHARE
NZ, NY, NX = 8, 4, 4


def params(mib):
    return pltpu.CompilerParams(vmem_limit_bytes=mib * 1024 * 1024)


def after(x, *deps):
    return lax.optimization_barrier((x,) + deps)[0]


def cost(flops, nbytes):
    return pl.CostEstimate(flops=flops, bytes_accessed=nbytes, transcendentals=0)


def vspec():
    return pl.BlockSpec(memory_space=pltpu.VMEM)


def hbm_spec():
    return pl.BlockSpec(memory_space=pltpu.HBM)


def nt_dot(a, b):
    return lax.dot_general(a, b, (((1,), (1,)), ((), ())), preferred_element_type=F32)


def tn_dot(a, b):
    return lax.dot_general(a, b, (((0,), (0,)), ((), ())), preferred_element_type=F32)


def left_lanes(wide):
    lane = lax.broadcasted_iota(jnp.int32, wide.shape, 1)
    return jnp.where(lane < 64, wide, 0.0)


def pair_tile(even, odd):
    lane = lax.broadcasted_iota(jnp.int32, even.shape, 1)
    return jnp.where(lane < 64, even, pltpu.roll(odd, 64, 1))


def half_tile(tile, odd):
    wide = tile.astype(F32)
    return jnp.where(odd == 1, pltpu.roll(wide, 64, 1), wide)


def unpack_rope(packed, core):
    row = lax.broadcasted_iota(jnp.int32, (SHARE, SHARE), 0)
    col = lax.broadcasted_iota(jnp.int32, (SHARE, SHARE), 1)
    pick = jnp.where(col == core * 8 + row // 2, 1.0, 0.0).astype(BF)
    wide = jnp.dot(pick, packed, preferred_element_type=F32)
    odd = lax.broadcasted_iota(jnp.int32, (SHARE, 128), 0) % 2 == 1
    return left_lanes(jnp.where(odd, pltpu.roll(wide, 64, 1), wide))


def pack_body(kv_ref, rope_ref, out_ref, lat, rope, sems):
    head = lax.axis_index("head")
    wide = kv_ref.at[:, pl.ds(pl.multiple_of(head * SHARE, SHARE), SHARE), :]
    thin = rope_ref.at[:, pl.ds(pl.multiple_of(head // 2 * SHARE, SHARE), SHARE), :]
    copies = (
        pltpu.make_async_copy(wide, lat, sems.at[0]),
        pltpu.make_async_copy(thin, rope, sems.at[1]),
    )
    for copy in copies:
        copy.start()
    for copy in copies:
        copy.wait()
    tiles = [lat[b, :, t * 128:(t + 1) * 128] for b in range(OWN) for t in range(TILES)]
    thin_rows = [unpack_rope(rope[b], head % 2) for b in range(OWN)]
    tiles += [pair_tile(*thin_rows[b:b + 2]).astype(BF) for b in range(0, OWN, 2)]
    for z in range(NZ):
        for n, tile in enumerate(tiles):
            at = z * SHARD_ROWS + n * SHARE
            out_ref[at:at + SHARE, :] = tile


def pack_call(kv, rope):
    return pl.pallas_call(
        pack_body,
        in_specs=[hbm_spec()] * 2,
        out_specs=vspec(),
        out_shape=jax.ShapeDtypeStruct((NZ * SHARD_ROWS, 128), BF),
        scratch_shapes=[
            pltpu.VMEM((OWN, SHARE, LAT), BF),
            pltpu.VMEM((OWN, SHARE, 128), BF),
            pltpu.SemaphoreType.DMA((2,)),
        ],
        compiler_params=params(56),
        name="pack_share",
    )(kv, rope)


def share_of(me, g):
    return (me // 2 + NX - g // 2) % NX, (me % 2 + g % 2) % 2


def prep_body(kv_hbm, rope_hbm, q_hbm, qr_hbm, g_hbm, own_out, q_out, g_out,
              kv_ref, rope_ref, qr_ref, sems):
    copies = [
        pltpu.make_async_copy(qr_hbm, qr_ref, sems.at[0]),
        pltpu.make_async_copy(rope_hbm, rope_ref, sems.at[1]),
        pltpu.make_async_copy(kv_hbm, kv_ref, sems.at[2]),
    ]
    for h in range(HEADS):
        cols, rows = pl.ds(h * LAT, LAT), pl.ds(h * 128, 128)
        copies.append(pltpu.make_async_copy(
            q_hbm.at[:, cols], q_out.at[rows, pl.ds(0, LAT)], sems.at[3 + 2 * h]))
        copies.append(pltpu.make_async_copy(
            g_hbm.at[:, cols], g_out.at[rows, :], sems.at[4 + 2 * h]))
    for copy in copies:
        copy.start()
    me = lax.axis_index("head")
    lane = lax.broadcasted_iota(jnp.int32, (128, 128), 1)
    copies[0].wait()
    for h in range(HEADS):
        pair = qr_ref[:, (h // 2) * 128:(h // 2 + 1) * 128].astype(F32)
        if h % 2:
            pair = pltpu.roll(pair, 64, 1)
        q_out[h * 128:(h + 1) * 128, LAT:] = jnp.where(lane < 64, pair, 0.0).astype(BF)
    copies[1].wait()
    for g in range(GROUPS):
        chip, core = share_of(me, g)
        for b in range(OWN):
            own_out[g, b * SHARE:(b + 1) * SHARE, LAT:] = unpack_rope(
                rope_ref[b, pl.ds(pl.multiple_of(chip * SHARE, SHARE), SHARE), :], core
            ).astype(BF)
    copies[2].wait()
    for g in range(GROUPS):
        chip, core = share_of(me, g)
        at = pl.multiple_of((chip * 2 + core) * SHARE, SHARE)
        for b in range(OWN):
            own_out[g, b * SHARE:(b + 1) * SHARE, :LAT] = kv_ref[b, pl.ds(at, SHARE), :]
    for copy in copies[3:]:
        copy.wait()


def prep_call(kv, rope, q, qr, g):
    return pl.pallas_call(
        prep_body,
        in_specs=[hbm_spec()] * 5,
        out_specs=[vspec()] * 3,
        out_shape=[
            jax.ShapeDtypeStruct((GROUPS, SPAN, WIDE), BF),
            jax.ShapeDtypeStruct((ROWS, WIDE), BF),
            jax.ShapeDtypeStruct((ROWS, LAT), BF),
        ],
        scratch_shapes=[
            pltpu.VMEM(kv.shape, BF),
            pltpu.VMEM(rope.shape, BF),
            pltpu.VMEM(qr.shape, BF),
            pltpu.SemaphoreType.DMA((3 + 2 * HEADS,)),
        ],
        compiler_params=params(10),
        cost_estimate=cost(1000, 10_000_000),
        name="prep_operands",
    )(kv, rope, q, qr, g)


def rows_at(ref, at, count):
    return ref[pl.ds(pl.multiple_of(at, SHARE), count), :]


def pick_y_body(*refs):
    wants, shards, outs = refs[:NY], refs[NY], refs[NY + 1:]
    ctx = lax.axis_index("ctx")
    for dy in range(NY):
        thin = []
        for r in range(NZ):
            z = (ctx // NY + NZ - r) % NZ
            w = jnp.maximum(wants[dy][z * NY + ctx % NY], 0)
            base = z * SHARD_ROWS
            outs[dy][r * BLOCK_ROWS:(r + 1) * BLOCK_ROWS, :] = rows_at(
                shards, base + w * BLOCK_ROWS, BLOCK_ROWS
            )
            tile = rows_at(shards, base + OWN * BLOCK_ROWS + w // 2 * SHARE, SHARE)
            thin.append(half_tile(tile, w % 2))
        for r in range(0, NZ, 2):
            at = COL_LAT + r // 2 * SHARE
            outs[dy][at:at + SHARE, :] = pair_tile(thin[r], thin[r + 1]).astype(BF)


def pick_y_call(wants, shards):
    return pl.pallas_call(
        pick_y_body,
        in_specs=[pl.BlockSpec(memory_space=pltpu.SMEM)] * NY + [vspec()],
        out_specs=[vspec()] * NY,
        out_shape=[jax.ShapeDtypeStruct((COL_ROWS, 128), BF)] * NY,
        compiler_params=params(4),
        name="pick_for_y_peers",
    )(*wants, shards)


def pick_x_body(src_ref, y0, y1, y2, y3, out_ref, stage):
    for dy, ref in enumerate((y0, y1, y2, y3)):
        stage[dy * COL_ROWS:(dy + 1) * COL_ROWS, :] = ref[...]
    thin = []
    for u in range(REMOTE):
        base, r = src_ref[u] // NZ * COL_ROWS, src_ref[u] % NZ
        out_ref[u * BLOCK_ROWS:(u + 1) * BLOCK_ROWS, :] = rows_at(
            stage, base + r * BLOCK_ROWS, BLOCK_ROWS
        )
        thin.append(half_tile(rows_at(stage, base + COL_LAT + r // 2 * SHARE, SHARE), r % 2))
    for u in range(0, REMOTE, 2):
        at = FAR_LAT + u // 2 * SHARE
        odd = thin[min(u + 1, REMOTE - 1)]
        out_ref[at:at + SHARE, :] = pair_tile(thin[u], odd).astype(BF)


def pick_x_call(src, cols):
    return pl.pallas_call(
        pick_x_body,
        in_specs=[pl.BlockSpec(memory_space=pltpu.SMEM)] + [vspec()] * NY,
        out_specs=vspec(),
        out_shape=jax.ShapeDtypeStruct((FAR_PACKED, 128), BF),
        scratch_shapes=[pltpu.VMEM((NY * COL_ROWS, 128), BF)],
        compiler_params=params(4),
        name="pick_selected",
    )(src, *cols)


def scores_body(me_ref, far_ref, pos_ref, x0, x1, x2, x3, c0, c1, c2, c3, own, q_ref, g_ref,
                k_out, p_out, ds_out, s_scr, e_scr, bias_scr):
    me = me_ref[0]
    pos = pos_ref[...] - me_ref[1]
    for u in range(REMOTE):
        line = jnp.broadcast_to(far_ref[u:u + 1, :], (SHARE, 128))
        for g in range(GROUPS):
            bias_scr[g * GROUP + u * SHARE:g * GROUP + (u + 1) * SHARE, :] = line
    step = lax.broadcasted_iota(jnp.int32, (SHARE, 128), 0)
    for g in range(GROUPS):
        chip, core = share_of(me, g)
        for b in range(OWN):
            at = g * GROUP + FAR_ROWS + b * SHARE
            key = step + (b * 128 + (chip * 2 + core) * SHARE)
            bias_scr[at:at + SHARE, :] = jnp.where(key <= pos, 0.0, NEG_FILL)
    for g, ref in enumerate((x0, c0, x1, c1, x2, c2, x3, c3)):
        for u in range(REMOTE):
            rows = slice(g * GROUP + u * SHARE, g * GROUP + (u + 1) * SHARE)
            for t in range(TILES):
                at = u * BLOCK_ROWS + t * SHARE
                k_out[rows, t * 128:(t + 1) * 128] = ref[at:at + SHARE, :]
            at = FAR_LAT + u // 2 * SHARE
            k_out[rows, LAT:] = left_lanes(half_tile(ref[at:at + SHARE, :], u % 2)).astype(BF)
        k_out[g * GROUP + FAR_ROWS:(g + 1) * GROUP, :] = own[g]

    def chunk(c, carry):
        at = c * CH
        q = q_ref[pl.ds(at, CH), :]
        g = g_ref[pl.ds(at, CH), :]
        top = jnp.full((1, CH), -jnp.inf, F32)
        for k in range(GROUPS):
            rows = slice(k * GROUP, (k + 1) * GROUP)
            bias = bias_scr[rows, :]
            s = nt_dot(k_out[rows, :], q) * (SCALE_FACTOR * LOG2E)
            s = s + jnp.concatenate([bias, bias], axis=1)
            s_scr[rows, :] = s
            top = jnp.maximum(top, jnp.max(s, axis=0, keepdims=True))
        total = jnp.zeros((1, CH), F32)
        delta = jnp.zeros((1, CH), F32)
        for k in range(GROUPS):
            rows = slice(k * GROUP, (k + 1) * GROUP)
            e = nt_dot(k_out[rows, :LAT], g)
            e_scr[rows, :] = e
            w = jnp.exp2(s_scr[rows, :] - top)
            s_scr[rows, :] = w
            total = total + jnp.sum(w, axis=0, keepdims=True)
            delta = delta + jnp.sum(w * e, axis=0, keepdims=True)
        inv = 1.0 / total
        delta = delta * inv
        for k in range(GROUPS):
            rows = slice(k * GROUP, (k + 1) * GROUP)
            p = s_scr[rows, :] * inv
            p_out[c, rows, :] = p.astype(BF)
            ds_out[c, rows, :] = ((e_scr[rows, :] - delta) * (p * SCALE_FACTOR)).astype(BF)
        return carry

    for c in range(NCH):
        chunk(c, 0)


def scores_call(me, far, pos, xs, cs, own, q, g):
    return pl.pallas_call(
        scores_body,
        in_specs=[pl.BlockSpec(memory_space=pltpu.SMEM)] + [vspec()] * 13,
        out_specs=[vspec()] * 3,
        out_shape=[
            jax.ShapeDtypeStruct((KEYS, WIDE), BF),
            jax.ShapeDtypeStruct((NCH, KEYS, CH), BF),
            jax.ShapeDtypeStruct((NCH, KEYS, CH), BF),
        ],
        scratch_shapes=[
            pltpu.VMEM((KEYS, CH), F32),
            pltpu.VMEM((KEYS, CH), F32),
            pltpu.VMEM((KEYS, 128), F32),
        ],
        compiler_params=params(30),
        cost_estimate=cost(2 * KEYS * ROWS * 1152, 16_000_000),
        name="scores",
    )(me, far, pos, *xs, *cs, own, q, g)


def dkv_body(p_ref, ds_ref, q_ref, g_ref, keep_ref, send_ref):
    for cr, out in enumerate((keep_ref, send_ref)):
        rows = slice(cr * GROUP, (cr + 1) * GROUP)
        ds = jnp.concatenate([ds_ref[c, rows, :] for c in range(NCH)], axis=1)
        p = jnp.concatenate([p_ref[c, rows, :] for c in range(NCH)], axis=1)
        a = jnp.dot(ds, q_ref[...], preferred_element_type=F32)
        b = jnp.dot(p, g_ref[...], preferred_element_type=F32)
        lat, thin = a[:, :LAT] + b, a[:, LAT:]
        for u in range(REMOTE + OWN):
            mine = slice(u * SHARE, (u + 1) * SHARE)
            for t in range(TILES):
                at = u * BLOCK_ROWS + t * SHARE
                out[at:at + SHARE, :] = lat[mine, t * 128:(t + 1) * 128].astype(out.dtype)
        for u in range(0, REMOTE + OWN, 2):
            at = GRAD_LAT + u // 2 * SHARE
            odd = min(u + 1, REMOTE + OWN - 1)
            pair = pair_tile(thin[u * SHARE:(u + 1) * SHARE], thin[odd * SHARE:(odd + 1) * SHARE])
            out[at:at + SHARE, :] = pair.astype(out.dtype)


def dkv_call(dx, p, ds, q, g):
    part = pl.BlockSpec((NCH, CHIP, CH), lambda i: (0, dx, 0))
    return pl.pallas_call(
        dkv_body,
        grid=(1,),
        in_specs=[part, part, pl.BlockSpec((ROWS, WIDE), lambda i: (0, 0)),
                  pl.BlockSpec((ROWS, LAT), lambda i: (0, 0))],
        out_specs=[pl.BlockSpec((GRAD_ROWS, 128), lambda i: (0, 0))] * 2,
        out_shape=[
            jax.ShapeDtypeStruct((GRAD_ROWS, 128), F32),
            jax.ShapeDtypeStruct((GRAD_ROWS, 128), BF),
        ],
        compiler_params=params(16),
        cost_estimate=cost(2 * CHIP * ROWS * 1152, 5_000_000),
        name=f"dkv_chunk{dx}",
    )(p, ds, q, g)


def dq_body(ds_ref, k_ref, lat_ref, rope_ref):
    res = tn_dot(ds_ref[0], k_ref[...])
    lat_ref[:, :LAT] = res[:128, :LAT].astype(BF)
    lat_ref[:, LAT:] = res[128:, :LAT].astype(BF)
    lane = lax.broadcasted_iota(jnp.int32, (128, 128), 1)
    odd = pltpu.roll(res[128:, LAT:], 64, 1)
    rope_ref[...] = jnp.where(lane < 64, res[:128, LAT:], odd).astype(BF)


def dq_call(ds, keys):
    return pl.pallas_call(
        dq_body,
        grid=(NCH,),
        in_specs=[
            pl.BlockSpec((1, KEYS, CH), lambda i: (i, 0, 0)),
            pl.BlockSpec((KEYS, WIDE), lambda i: (0, 0)),
        ],
        out_specs=[
            pl.BlockSpec((128, 2 * LAT), lambda i: (0, i)),
            pl.BlockSpec((128, 128), lambda i: (0, i)),
        ],
        out_shape=[
            jax.ShapeDtypeStruct((128, HEADS * LAT), BF),
            jax.ShapeDtypeStruct((128, HEADS * 64), BF),
        ],
        compiler_params=params(14),
        cost_estimate=cost(2 * KEYS * ROWS * 640, 8_000_000),
        name="dq",
    )(ds, keys)


def slots_body(at_ref, want_ref, keep_ref, swap_ref, r1_ref, r2_ref, r3_ref,
               slot_out, own_out, far):
    total = keep_ref[...] + swap_ref[...].astype(F32)
    for ref in (r1_ref, r2_ref, r3_ref):
        total = total + ref[...].astype(F32)
    far[...] = total
    for b in range(OWN):
        u, rows = REMOTE + b, slice(b * SHARE, (b + 1) * SHARE)
        for t in range(TILES):
            at = u * BLOCK_ROWS + t * SHARE
            own_out[rows, t * 128:(t + 1) * 128] = far[at:at + SHARE, :]
        at = GRAD_LAT + u // 2 * SHARE
        own_out[rows, LAT:] = left_lanes(half_tile(far[at:at + SHARE, :], u % 2))
    lane = lax.broadcasted_iota(jnp.int32, (SHARE, 128), 1)
    for c in range(SLOTS):
        rows = slice(c * SHARE, (c + 1) * SHARE)
        w = want_ref[c]
        flag = jnp.where(w >= 0, 64 + w, 128)
        u = at_ref[c]
        for t in range(TILES):
            tile = rows_at(far, u * BLOCK_ROWS + t * SHARE, SHARE)
            slot_out[rows, t * 128:(t + 1) * 128] = tile.astype(BF)
        thin = left_lanes(half_tile(rows_at(far, GRAD_LAT + u // 2 * SHARE, SHARE), u % 2))
        slot_out[rows, LAT:] = jnp.where(lane == flag, 1.0, thin).astype(BF)


def slots_call(at, want, keep, swap, r1, r2, r3):
    smem = pl.BlockSpec(memory_space=pltpu.SMEM)
    return pl.pallas_call(
        slots_body,
        in_specs=[smem, smem] + [vspec()] * 5,
        out_specs=[vspec()] * 2,
        out_shape=[
            jax.ShapeDtypeStruct((SLOTS * SHARE, WIDE), BF),
            jax.ShapeDtypeStruct((SPAN, WIDE), F32),
        ],
        scratch_shapes=[pltpu.VMEM((GRAD_ROWS, 128), F32)],
        compiler_params=params(8),
        name="fill_slots",
    )(at, want, keep, swap, r1, r2, r3)


def finish_body(own_ref, back_ref, lat_ref, rope_ref, acc, scr):
    acc[...] = own_ref[...]
    for c in range(SLOTS):
        piece = back_ref[c * SHARE:(c + 1) * SHARE, :].astype(F32)
        for b in range(OWN):
            mine = piece[:, LAT + 64 + b:LAT + 65 + b] > 0.5
            acc[b * SHARE:(b + 1) * SHARE, :] += jnp.where(mine, piece, 0.0)
    for b in range(OWN):
        lat_ref[b] = acc[b * SHARE:(b + 1) * SHARE, :LAT]
    scr[...] = acc[:, LAT:]
    half = SPAN // 2
    even = scr[pl.ds(0, half, 2), :]
    odd = scr[pl.ds(1, half, 2), :]
    lane = lax.broadcasted_iota(jnp.int32, (half, 128), 1)
    both = jnp.where(lane < 64, even, pltpu.roll(odd, 64, 1))
    rope_ref[...] = both.reshape(OWN, SHARE // 2, 128)


def finish_call(own, back):
    return pl.pallas_call(
        finish_body,
        in_specs=[vspec()] * 2,
        out_specs=[vspec()] * 2,
        out_shape=[
            jax.ShapeDtypeStruct((OWN, SHARE, LAT), F32),
            jax.ShapeDtypeStruct((OWN, SHARE // 2, 128), F32),
        ],
        scratch_shapes=[pltpu.VMEM((SPAN, WIDE), F32), pltpu.VMEM((SPAN, 128), F32)],
        compiler_params=params(8),
        name="finish",
    )(own, back)


def step_z(a, d):
    return lax.ppermute(a, "ctx", [(i, (i + NY * d) % (NZ * NY)) for i in range(NZ * NY)])


def step_y(a, d):
    return lax.ppermute(
        a, "ctx", [(z * NY + y, z * NY + (y + d) % NY) for z in range(NZ) for y in range(NY)]
    )


def step_x(a, d):
    return lax.ppermute(a, "head", [(i, (i + 2 * d) % (2 * NX)) for i in range(2 * NX)])


def swap_core(a):
    return lax.ppermute(a, "head", [(i, i ^ 1) for i in range(2 * NX)])


def local(q_latent, q_rope, out_grad, kv_latent, key_rope, block_lists, query_pos):
    ctx = lax.axis_index("ctx")
    head = lax.axis_index("head")
    my_z, my_y = ctx // NY, ctx % NY
    me = jnp.stack([head, ctx * (OWN * 128)]).astype(jnp.int32)

    shard = pack_call(kv_latent, key_rope)
    columns = [[z * NY + y for z in range(NZ)] for y in range(NY)]
    shards = lax.all_to_all(shard, "ctx", 0, 0, tiled=True, axis_index_groups=columns)

    block_lists, me, query_pos = after((block_lists, me, query_pos), shard)
    every = jnp.arange(NZ * NY * OWN, dtype=jnp.int32)
    present = jnp.any(block_lists.reshape(-1)[:, None] == every[None, :], axis=0)
    remote = present & (every // OWN != ctx)
    grid = remote.reshape(NZ * NY, OWN)
    want = jnp.max(jnp.where(grid, jnp.arange(OWN, dtype=jnp.int32)[None, :], -1), axis=1)
    rank = jnp.cumsum(remote.astype(jnp.int32)) - 1
    slot_ids = jnp.arange(16, dtype=jnp.int32)
    match = remote[None, :] & (rank[None, :] == slot_ids[:, None])
    remote_ids = jnp.max(jnp.where(match, every[None, :], -1), axis=1)
    owner = jnp.maximum(remote_ids, 0) // OWN
    src = jnp.where(
        remote_ids >= 0, ((my_y - owner % NY) % NY) * NZ + (my_z - owner // NY) % NZ, 0
    ).astype(jnp.int32)
    ctxs = jnp.arange(SLOTS, dtype=jnp.int32)
    hit = (remote_ids[None, :] >= 0) & (remote_ids[None, :] // OWN == ctxs[:, None])
    back_at = jnp.sum(jnp.where(hit, slot_ids[None, :], 0), axis=1).astype(jnp.int32)
    wants = [want] + [step_y(want, -d) for d in range(1, NY)]
    chosen = jnp.any(block_lists[:, None, :] == remote_ids[None, :, None], axis=2)
    chosen = chosen & (remote_ids >= 0)[None, :]
    far_bias = jnp.where(chosen, 0.0, NEG_FILL).astype(F32).T

    cols = pick_y_call(wants, shards)
    cols = [cols[0]] + [step_y(cols[d], d) for d in range(1, NY)]
    x0 = pick_x_call(src, cols)
    x2, x1, x3 = step_x(x0, 2), step_x(x0, 1), step_x(x0, -1)
    xs = [x0, x1, x2, x3]
    arrays = after((kv_latent, key_rope, q_latent, q_rope, out_grad), x0)
    own_keys, q, g = prep_call(*arrays)
    cs = [swap_core(x0)] + [swap_core(after(a, own_keys)) for a in xs[1:]]

    keys, p, ds = scores_call(me, far_bias, query_pos.reshape(1, -1), xs, cs, own_keys, q, g)

    order = (2, 1, 3, 0)
    keep, send, part, got = {}, {}, {}, {}
    for n, dx in enumerate(order):
        keep[dx], send[dx] = dkv_call(dx, p, ds, q, g)
        p, ds = after((p, ds), send[dx])
        if n:
            prev = order[n - 1]
            part[prev] = (keep[prev] + swap_core(send[prev]).astype(F32)).astype(BF)
            got[prev] = step_x(part[prev], -prev)
            p, ds = after((p, ds), part[prev])
    swap = swap_core(send[0])
    dq_latent, dq_rope = dq_call(ds, keys)
    mine, dq_latent, dq_rope = lax.optimization_barrier((keep[0], dq_latent, dq_rope))

    slots, own = slots_call(back_at, want, mine, swap, got[1], got[2], got[3])
    back = lax.all_to_all(slots, "ctx", split_axis=0, concat_axis=0, tiled=True)
    dkv_latent, dkey_rope = finish_call(own, back)
    return (dq_latent, dq_rope, dkv_latent, dkey_rope)


def solution(mesh):
    return jax.shard_map(
        local,
        mesh=mesh,
        in_specs=(
            P("ctx", "head"),
            P("ctx", "head"),
            P("ctx", "head"),
            P("ctx", None, None),
            P("ctx", None, None),
            P("ctx", None),
            P("ctx"),
        ),
        out_specs=(
            P("ctx", "head"),
            P("ctx", "head"),
            P("ctx", "head", None),
            P("ctx", "head", None),
        ),
        check_vma=False,
    )
```

```python
import functools

import jax
import jax.numpy as jnp
from jax import lax
from jax.experimental import pallas as pl
from jax.experimental.pallas import tpu as pltpu
from jax.sharding import PartitionSpec as P

SCALE_FACTOR = 192.0 ** (-0.5)
LOG2E = 1.4426950408889634
NEG_FILL = -1e30
BF = jnp.bfloat16
F32 = jnp.float32
LAT = 512
WIDE = 640
SHARE = 16
REMOTE = 13
OWN = 4
FAR_ROWS = REMOTE * SHARE
GROUP = (REMOTE + OWN) * SHARE
GROUPS = 8
KEYS = GROUP * GROUPS
CHIP = 2 * GROUP
HEADS = 8
ROWS = 1024
CH = 256
NCH = ROWS // CH
SPAN = OWN * SHARE
SLOTS = 32
TILES = LAT // 128
BLOCK_ROWS = TILES * SHARE
SHARD_ROWS = OWN * BLOCK_ROWS + OWN // 2 * SHARE
COL_LAT = 8 * BLOCK_ROWS
COL_ROWS = COL_LAT + 4 * SHARE
FAR_LAT = REMOTE * BLOCK_ROWS
FAR_PACKED = FAR_LAT + (REMOTE + 1) // 2 * SHARE
GRAD_LAT = (REMOTE + OWN) * BLOCK_ROWS
GRAD_ROWS = GRAD_LAT + (REMOTE + OWN + 1) // 2 * SHARE
NZ, NY, NX = 8, 4, 4


def params(mib):
    return pltpu.CompilerParams(vmem_limit_bytes=mib * 1024 * 1024)


def after(x, *deps):
    return lax.optimization_barrier((x,) + deps)[0]


def cost(flops, nbytes):
    return pl.CostEstimate(flops=flops, bytes_accessed=nbytes, transcendentals=0)


def vspec():
    return pl.BlockSpec(memory_space=pltpu.VMEM)


def hbm_spec():
    return pl.BlockSpec(memory_space=pltpu.HBM)


def nt_dot(a, b):
    return lax.dot_general(a, b, (((1,), (1,)), ((), ())), preferred_element_type=F32)


def tn_dot(a, b):
    return lax.dot_general(a, b, (((0,), (0,)), ((), ())), preferred_element_type=F32)


def left_lanes(wide):
    lane = lax.broadcasted_iota(jnp.int32, wide.shape, 1)
    return jnp.where(lane < 64, wide, 0.0)


def pair_tile(even, odd):
    lane = lax.broadcasted_iota(jnp.int32, even.shape, 1)
    return jnp.where(lane < 64, even, pltpu.roll(odd, 64, 1))


def half_tile(tile, odd):
    wide = tile.astype(F32)
    return jnp.where(odd == 1, pltpu.roll(wide, 64, 1), wide)


def unpack_rope(packed, core):
    row = lax.broadcasted_iota(jnp.int32, (SHARE, SHARE), 0)
    col = lax.broadcasted_iota(jnp.int32, (SHARE, SHARE), 1)
    pick = jnp.where(col == core * 8 + row // 2, 1.0, 0.0).astype(BF)
    wide = jnp.dot(pick, packed, preferred_element_type=F32)
    odd = lax.broadcasted_iota(jnp.int32, (SHARE, 128), 0) % 2 == 1
    return left_lanes(jnp.where(odd, pltpu.roll(wide, 64, 1), wide))


def pack_body(kv_ref, rope_ref, out_ref, lat, rope, sems):
    head = lax.axis_index("head")
    wide = kv_ref.at[:, pl.ds(pl.multiple_of(head * SHARE, SHARE), SHARE), :]
    thin = rope_ref.at[:, pl.ds(pl.multiple_of(head // 2 * SHARE, SHARE), SHARE), :]
    copies = (
        pltpu.make_async_copy(wide, lat, sems.at[0]),
        pltpu.make_async_copy(thin, rope, sems.at[1]),
    )
    for copy in copies:
        copy.start()
    for copy in copies:
        copy.wait()
    tiles = [lat[b, :, t * 128:(t + 1) * 128] for b in range(OWN) for t in range(TILES)]
    thin_rows = [unpack_rope(rope[b], head % 2) for b in range(OWN)]
    tiles += [pair_tile(*thin_rows[b:b + 2]).astype(BF) for b in range(0, OWN, 2)]
    for z in range(NZ):
        for n, tile in enumerate(tiles):
            at = z * SHARD_ROWS + n * SHARE
            out_ref[at:at + SHARE, :] = tile


def pack_call(kv, rope):
    return pl.pallas_call(
        pack_body,
        in_specs=[hbm_spec()] * 2,
        out_specs=vspec(),
        out_shape=jax.ShapeDtypeStruct((NZ * SHARD_ROWS, 128), BF),
        scratch_shapes=[
            pltpu.VMEM((OWN, SHARE, LAT), BF),
            pltpu.VMEM((OWN, SHARE, 128), BF),
            pltpu.SemaphoreType.DMA((2,)),
        ],
        compiler_params=params(56),
        name="pack_share",
    )(kv, rope)


def share_of(me, g):
    return (me // 2 + NX - g // 2) % NX, (me % 2 + g % 2) % 2


def prep_body(kv_hbm, rope_hbm, q_hbm, qr_hbm, g_hbm, own_out, q_out, g_out,
              kv_ref, rope_ref, qr_ref, sems):
    copies = [
        pltpu.make_async_copy(qr_hbm, qr_ref, sems.at[0]),
        pltpu.make_async_copy(rope_hbm, rope_ref, sems.at[1]),
        pltpu.make_async_copy(kv_hbm, kv_ref, sems.at[2]),
    ]
    for h in range(HEADS):
        cols, rows = pl.ds(h * LAT, LAT), pl.ds(h * 128, 128)
        copies.append(pltpu.make_async_copy(
            q_hbm.at[:, cols], q_out.at[rows, pl.ds(0, LAT)], sems.at[3 + 2 * h]))
        copies.append(pltpu.make_async_copy(
            g_hbm.at[:, cols], g_out.at[rows, :], sems.at[4 + 2 * h]))
    for copy in copies:
        copy.start()
    me = lax.axis_index("head")
    lane = lax.broadcasted_iota(jnp.int32, (128, 128), 1)
    copies[0].wait()
    for h in range(HEADS):
        pair = qr_ref[:, (h // 2) * 128:(h // 2 + 1) * 128].astype(F32)
        if h % 2:
            pair = pltpu.roll(pair, 64, 1)
        q_out[h * 128:(h + 1) * 128, LAT:] = jnp.where(lane < 64, pair, 0.0).astype(BF)
    copies[1].wait()
    for g in range(GROUPS):
        chip, core = share_of(me, g)
        for b in range(OWN):
            own_out[g, b * SHARE:(b + 1) * SHARE, LAT:] = unpack_rope(
                rope_ref[b, pl.ds(pl.multiple_of(chip * SHARE, SHARE), SHARE), :], core
            ).astype(BF)
    copies[2].wait()
    for g in range(GROUPS):
        chip, core = share_of(me, g)
        at = pl.multiple_of((chip * 2 + core) * SHARE, SHARE)
        for b in range(OWN):
            own_out[g, b * SHARE:(b + 1) * SHARE, :LAT] = kv_ref[b, pl.ds(at, SHARE), :]
    for copy in copies[3:]:
        copy.wait()


def prep_call(kv, rope, q, qr, g):
    return pl.pallas_call(
        prep_body,
        in_specs=[hbm_spec()] * 5,
        out_specs=[vspec()] * 3,
        out_shape=[
            jax.ShapeDtypeStruct((GROUPS, SPAN, WIDE), BF),
            jax.ShapeDtypeStruct((ROWS, WIDE), BF),
            jax.ShapeDtypeStruct((ROWS, LAT), BF),
        ],
        scratch_shapes=[
            pltpu.VMEM(kv.shape, BF),
            pltpu.VMEM(rope.shape, BF),
            pltpu.VMEM(qr.shape, BF),
            pltpu.SemaphoreType.DMA((3 + 2 * HEADS,)),
        ],
        compiler_params=params(10),
        cost_estimate=cost(1000, 10_000_000),
        name="prep_operands",
    )(kv, rope, q, qr, g)


def rows_at(ref, at, count):
    return ref[pl.ds(pl.multiple_of(at, SHARE), count), :]


def pick_y_body(*refs):
    wants, shards, outs = refs[:NY], refs[NY], refs[NY + 1:]
    ctx = lax.axis_index("ctx")
    for dy in range(NY):
        thin = []
        for r in range(NZ):
            z = (ctx // NY + NZ - r) % NZ
            w = jnp.maximum(wants[dy][z * NY + ctx % NY], 0)
            base = z * SHARD_ROWS
            outs[dy][r * BLOCK_ROWS:(r + 1) * BLOCK_ROWS, :] = rows_at(
                shards, base + w * BLOCK_ROWS, BLOCK_ROWS
            )
            tile = rows_at(shards, base + OWN * BLOCK_ROWS + w // 2 * SHARE, SHARE)
            thin.append(half_tile(tile, w % 2))
        for r in range(0, NZ, 2):
            at = COL_LAT + r // 2 * SHARE
            outs[dy][at:at + SHARE, :] = pair_tile(thin[r], thin[r + 1]).astype(BF)


def pick_y_call(wants, shards):
    return pl.pallas_call(
        pick_y_body,
        in_specs=[pl.BlockSpec(memory_space=pltpu.SMEM)] * NY + [vspec()],
        out_specs=[vspec()] * NY,
        out_shape=[jax.ShapeDtypeStruct((COL_ROWS, 128), BF)] * NY,
        compiler_params=params(4),
        name="pick_for_y_peers",
    )(*wants, shards)


def pick_x_body(src_ref, y0, y1, y2, y3, out_ref, stage):
    for dy, ref in enumerate((y0, y1, y2, y3)):
        stage[dy * COL_ROWS:(dy + 1) * COL_ROWS, :] = ref[...]
    thin = []
    for u in range(REMOTE):
        base, r = src_ref[u] // NZ * COL_ROWS, src_ref[u] % NZ
        out_ref[u * BLOCK_ROWS:(u + 1) * BLOCK_ROWS, :] = rows_at(
            stage, base + r * BLOCK_ROWS, BLOCK_ROWS
        )
        thin.append(half_tile(rows_at(stage, base + COL_LAT + r // 2 * SHARE, SHARE), r % 2))
    for u in range(0, REMOTE, 2):
        at = FAR_LAT + u // 2 * SHARE
        odd = thin[min(u + 1, REMOTE - 1)]
        out_ref[at:at + SHARE, :] = pair_tile(thin[u], odd).astype(BF)


def pick_x_call(src, cols):
    return pl.pallas_call(
        pick_x_body,
        in_specs=[pl.BlockSpec(memory_space=pltpu.SMEM)] + [vspec()] * NY,
        out_specs=vspec(),
        out_shape=jax.ShapeDtypeStruct((FAR_PACKED, 128), BF),
        scratch_shapes=[pltpu.VMEM((NY * COL_ROWS, 128), BF)],
        compiler_params=params(4),
        name="pick_selected",
    )(src, *cols)


def log_scores(keys, q, bias):
    s = nt_dot(keys, q) * (SCALE_FACTOR * LOG2E)
    return s + jnp.concatenate([bias, bias], axis=1)


def fill_far(refs, k_out, starts):
    for ref, start in zip(refs, starts):
        for u in range(REMOTE):
            rows = slice(start + u * SHARE, start + (u + 1) * SHARE)
            for t in range(TILES):
                at = u * BLOCK_ROWS + t * SHARE
                k_out[rows, t * 128:(t + 1) * 128] = ref[at:at + SHARE, :]
            at = FAR_LAT + u // 2 * SHARE
            k_out[rows, LAT:] = left_lanes(half_tile(ref[at:at + SHARE, :], u % 2)).astype(BF)


def fill_far_bias(far_ref, bias_scr):
    for u in range(REMOTE):
        bias_scr[u * SHARE:(u + 1) * SHARE, :] = jnp.broadcast_to(
            far_ref[u:u + 1, :], (SHARE, 128)
        )


def far_scores_body(far_ref, x_ref, c_ref, q_ref, k_out, s_out, top_out, bias_scr):
    fill_far((x_ref, c_ref), k_out, (0, FAR_ROWS))
    fill_far_bias(far_ref, bias_scr)
    for c in range(NCH):
        q = q_ref[c * CH:(c + 1) * CH, :]
        top = jnp.full((1, CH), -jnp.inf, F32)
        for cr in range(2):
            rows = slice(cr * FAR_ROWS, (cr + 1) * FAR_ROWS)
            s = log_scores(k_out[rows, :], q, bias_scr[...])
            s_out[c, rows, :] = s
            top = jnp.maximum(top, jnp.max(s, axis=0, keepdims=True))
        top_out[c] = top


def far_scores_call(far, x, c, q):
    return pl.pallas_call(
        far_scores_body,
        in_specs=[vspec()] * 4,
        out_specs=[vspec()] * 3,
        out_shape=[
            jax.ShapeDtypeStruct((2 * FAR_ROWS, WIDE), BF),
            jax.ShapeDtypeStruct((NCH, 2 * FAR_ROWS, CH), F32),
            jax.ShapeDtypeStruct((NCH, 1, CH), F32),
        ],
        scratch_shapes=[pltpu.VMEM((FAR_ROWS, 128), F32)],
        compiler_params=params(10),
        cost_estimate=cost(2 * 2 * FAR_ROWS * ROWS * 640, 4_000_000),
        name="far_scores",
    )(far, x, c, q)


def own_scores_body(me_ref, pos_ref, own_ref, q_ref, s_out, top_out, bias_scr):
    pos = pos_ref[...] - me_ref[1]
    step = lax.broadcasted_iota(jnp.int32, (SHARE, 128), 0)
    for g in range(GROUPS):
        chip, core = share_of(me_ref[0], g)
        for b in range(OWN):
            at = g * SPAN + b * SHARE
            key = step + (b * 128 + (chip * 2 + core) * SHARE)
            bias_scr[at:at + SHARE, :] = jnp.where(key <= pos, 0.0, NEG_FILL)
    for c in range(NCH):
        q = q_ref[c * CH:(c + 1) * CH, :]
        top = jnp.full((1, CH), -jnp.inf, F32)
        for n in range(2):
            rows = slice(n * 4 * SPAN, (n + 1) * 4 * SPAN)
            keys = own_ref[4 * n:4 * n + 4].reshape(4 * SPAN, WIDE)
            s = log_scores(keys, q, bias_scr[rows, :])
            s_out[c, rows, :] = s
            top = jnp.maximum(top, jnp.max(s, axis=0, keepdims=True))
        top_out[c] = top


def own_scores_call(me, pos, own, q):
    return pl.pallas_call(
        own_scores_body,
        in_specs=[pl.BlockSpec(memory_space=pltpu.SMEM)] + [vspec()] * 3,
        out_specs=[vspec()] * 2,
        out_shape=[
            jax.ShapeDtypeStruct((NCH, GROUPS * SPAN, CH), F32),
            jax.ShapeDtypeStruct((NCH, 1, CH), F32),
        ],
        scratch_shapes=[pltpu.VMEM((GROUPS * SPAN, 128), F32)],
        compiler_params=params(10),
        cost_estimate=cost(2 * GROUPS * SPAN * ROWS * 640, 4_000_000),
        name="own_scores",
    )(me, pos, own, q)


EARLY = (0,)
LATE = tuple(dx for dx in range(NX) if dx not in EARLY)


def scores_body(far_ref, own, own_s, own_top, *refs):
    done = {dx: refs[3 * n:3 * n + 3] for n, dx in enumerate(EARLY)}
    refs = refs[3 * len(EARLY):]
    late = {dx: refs[2 * n:2 * n + 2] for n, dx in enumerate(LATE)}
    q_ref, g_ref, k_out, p_out, ds_out, s_scr, e_scr, bias_scr = refs[2 * len(LATE):]
    fill_far_bias(far_ref, bias_scr)
    for g in range(GROUPS):
        at, dx, cr = g * GROUP, g // 2, g % 2
        if dx in done:
            k_out[at:at + FAR_ROWS, :] = done[dx][0][cr * FAR_ROWS:(cr + 1) * FAR_ROWS, :]
        else:
            fill_far(late[dx][cr:cr + 1], k_out, (at,))
        k_out[at + FAR_ROWS:at + GROUP, :] = own[g]

    for c in range(NCH):
        q = q_ref[c * CH:(c + 1) * CH, :]
        grad = g_ref[c * CH:(c + 1) * CH, :]
        top = own_top[c]
        for dx in EARLY:
            top = jnp.maximum(top, done[dx][2][c])
        for dx in LATE:
            for g in (2 * dx, 2 * dx + 1):
                rows = slice(g * GROUP, g * GROUP + FAR_ROWS)
                s = log_scores(k_out[rows, :], q, bias_scr[...])
                s_scr[rows, :] = s
                top = jnp.maximum(top, jnp.max(s, axis=0, keepdims=True))
        total = jnp.zeros((1, CH), F32)
        delta = jnp.zeros((1, CH), F32)
        for g in range(GROUPS):
            at, dx, cr = g * GROUP, g // 2, g % 2
            rows = slice(at, at + GROUP)
            e = nt_dot(k_out[rows, :LAT], grad)
            e_scr[rows, :] = e
            if dx in done:
                far = done[dx][1][c, cr * FAR_ROWS:(cr + 1) * FAR_ROWS, :]
            else:
                far = s_scr[at:at + FAR_ROWS, :]
            s = jnp.concatenate([far, own_s[c, g * SPAN:(g + 1) * SPAN, :]], axis=0)
            w = jnp.exp2(s - top)
            s_scr[rows, :] = w
            total = total + jnp.sum(w, axis=0, keepdims=True)
            delta = delta + jnp.sum(w * e, axis=0, keepdims=True)
        inv = 1.0 / total
        delta = delta * inv
        for g in range(GROUPS):
            rows = slice(g * GROUP, (g + 1) * GROUP)
            p = s_scr[rows, :] * inv
            p_out[c, rows, :] = p.astype(BF)
            ds_out[c, rows, :] = ((e_scr[rows, :] - delta) * (p * SCALE_FACTOR)).astype(BF)


def scores_call(far, own, own_s, own_top, parts, q, g):
    return pl.pallas_call(
        scores_body,
        in_specs=[vspec()] * (4 + len(parts) + 2),
        out_specs=[vspec()] * 3,
        out_shape=[
            jax.ShapeDtypeStruct((KEYS, WIDE), BF),
            jax.ShapeDtypeStruct((NCH, KEYS, CH), BF),
            jax.ShapeDtypeStruct((NCH, KEYS, CH), BF),
        ],
        scratch_shapes=[
            pltpu.VMEM((KEYS, CH), F32),
            pltpu.VMEM((KEYS, CH), F32),
            pltpu.VMEM((FAR_ROWS, 128), F32),
        ],
        compiler_params=params(30),
        cost_estimate=cost(2 * KEYS * ROWS * 1152, 16_000_000),
        name="scores",
    )(far, own, own_s, own_top, *parts, q, g)


def dkv_body(p_ref, ds_ref, q_ref, g_ref, keep_ref, send_ref):
    for cr, out in enumerate((keep_ref, send_ref)):
        rows = slice(cr * GROUP, (cr + 1) * GROUP)
        ds = jnp.concatenate([ds_ref[c, rows, :] for c in range(NCH)], axis=1)
        p = jnp.concatenate([p_ref[c, rows, :] for c in range(NCH)], axis=1)
        a = jnp.dot(ds, q_ref[...], preferred_element_type=F32)
        b = jnp.dot(p, g_ref[...], preferred_element_type=F32)
        lat, thin = a[:, :LAT] + b, a[:, LAT:]
        for u in range(REMOTE + OWN):
            mine = slice(u * SHARE, (u + 1) * SHARE)
            for t in range(TILES):
                at = u * BLOCK_ROWS + t * SHARE
                out[at:at + SHARE, :] = lat[mine, t * 128:(t + 1) * 128].astype(out.dtype)
        for u in range(0, REMOTE + OWN, 2):
            at = GRAD_LAT + u // 2 * SHARE
            odd = min(u + 1, REMOTE + OWN - 1)
            pair = pair_tile(thin[u * SHARE:(u + 1) * SHARE], thin[odd * SHARE:(odd + 1) * SHARE])
            out[at:at + SHARE, :] = pair.astype(out.dtype)


def dkv_call(dx, p, ds, q, g):
    part = pl.BlockSpec((NCH, CHIP, CH), lambda i: (0, dx, 0))
    return pl.pallas_call(
        dkv_body,
        grid=(1,),
        in_specs=[part, part, pl.BlockSpec((ROWS, WIDE), lambda i: (0, 0)),
                  pl.BlockSpec((ROWS, LAT), lambda i: (0, 0))],
        out_specs=[pl.BlockSpec((GRAD_ROWS, 128), lambda i: (0, 0))] * 2,
        out_shape=[
            jax.ShapeDtypeStruct((GRAD_ROWS, 128), F32),
            jax.ShapeDtypeStruct((GRAD_ROWS, 128), BF),
        ],
        compiler_params=params(16),
        cost_estimate=cost(2 * CHIP * ROWS * 1152, 5_000_000),
        name=f"dkv_chunk{dx}",
    )(p, ds, q, g)


def dq_body(ds_ref, k_ref, lat_ref, rope_ref):
    res = tn_dot(ds_ref[0], k_ref[...])
    lat_ref[:, :LAT] = res[:128, :LAT].astype(BF)
    lat_ref[:, LAT:] = res[128:, :LAT].astype(BF)
    lane = lax.broadcasted_iota(jnp.int32, (128, 128), 1)
    odd = pltpu.roll(res[128:, LAT:], 64, 1)
    rope_ref[...] = jnp.where(lane < 64, res[:128, LAT:], odd).astype(BF)


def dq_call(ds, keys):
    return pl.pallas_call(
        dq_body,
        grid=(NCH,),
        in_specs=[
            pl.BlockSpec((1, KEYS, CH), lambda i: (i, 0, 0)),
            pl.BlockSpec((KEYS, WIDE), lambda i: (0, 0)),
        ],
        out_specs=[
            pl.BlockSpec((128, 2 * LAT), lambda i: (0, i)),
            pl.BlockSpec((128, 128), lambda i: (0, i)),
        ],
        out_shape=[
            jax.ShapeDtypeStruct((128, HEADS * LAT), BF),
            jax.ShapeDtypeStruct((128, HEADS * 64), BF),
        ],
        compiler_params=params(14),
        cost_estimate=cost(2 * KEYS * ROWS * 640, 8_000_000),
        name="dq",
    )(ds, keys)


def slots_body(at_ref, want_ref, keep_ref, swap_ref, r1_ref, r2_ref, r3_ref,
               slot_out, own_out, far):
    total = keep_ref[...] + swap_ref[...].astype(F32)
    for ref in (r1_ref, r2_ref, r3_ref):
        total = total + ref[...].astype(F32)
    far[...] = total
    for b in range(OWN):
        u, rows = REMOTE + b, slice(b * SHARE, (b + 1) * SHARE)
        for t in range(TILES):
            at = u * BLOCK_ROWS + t * SHARE
            own_out[rows, t * 128:(t + 1) * 128] = far[at:at + SHARE, :]
        at = GRAD_LAT + u // 2 * SHARE
        own_out[rows, LAT:] = left_lanes(half_tile(far[at:at + SHARE, :], u % 2))
    lane = lax.broadcasted_iota(jnp.int32, (SHARE, 128), 1)
    for c in range(SLOTS):
        rows = slice(c * SHARE, (c + 1) * SHARE)
        w = want_ref[c]
        flag = jnp.where(w >= 0, 64 + w, 128)
        u = at_ref[c]
        for t in range(TILES):
            tile = rows_at(far, u * BLOCK_ROWS + t * SHARE, SHARE)
            slot_out[rows, t * 128:(t + 1) * 128] = tile.astype(BF)
        thin = left_lanes(half_tile(rows_at(far, GRAD_LAT + u // 2 * SHARE, SHARE), u % 2))
        slot_out[rows, LAT:] = jnp.where(lane == flag, 1.0, thin).astype(BF)


def slots_call(at, want, keep, swap, r1, r2, r3):
    smem = pl.BlockSpec(memory_space=pltpu.SMEM)
    return pl.pallas_call(
        slots_body,
        in_specs=[smem, smem] + [vspec()] * 5,
        out_specs=[vspec()] * 2,
        out_shape=[
            jax.ShapeDtypeStruct((SLOTS * SHARE, WIDE), BF),
            jax.ShapeDtypeStruct((SPAN, WIDE), F32),
        ],
        scratch_shapes=[pltpu.VMEM((GRAD_ROWS, 128), F32)],
        compiler_params=params(8),
        name="fill_slots",
    )(at, want, keep, swap, r1, r2, r3)


def finish_body(own_ref, back_ref, lat_ref, rope_ref, acc, scr):
    acc[...] = own_ref[...]
    for c in range(SLOTS):
        piece = back_ref[c * SHARE:(c + 1) * SHARE, :].astype(F32)
        for b in range(OWN):
            mine = piece[:, LAT + 64 + b:LAT + 65 + b] > 0.5
            acc[b * SHARE:(b + 1) * SHARE, :] += jnp.where(mine, piece, 0.0)
    for b in range(OWN):
        lat_ref[b] = acc[b * SHARE:(b + 1) * SHARE, :LAT]
    scr[...] = acc[:, LAT:]
    half = SPAN // 2
    even = scr[pl.ds(0, half, 2), :]
    odd = scr[pl.ds(1, half, 2), :]
    lane = lax.broadcasted_iota(jnp.int32, (half, 128), 1)
    both = jnp.where(lane < 64, even, pltpu.roll(odd, 64, 1))
    rope_ref[...] = both.reshape(OWN, SHARE // 2, 128)


def finish_call(own, back):
    return pl.pallas_call(
        finish_body,
        in_specs=[vspec()] * 2,
        out_specs=[vspec()] * 2,
        out_shape=[
            jax.ShapeDtypeStruct((OWN, SHARE, LAT), F32),
            jax.ShapeDtypeStruct((OWN, SHARE // 2, 128), F32),
        ],
        scratch_shapes=[pltpu.VMEM((SPAN, WIDE), F32), pltpu.VMEM((SPAN, 128), F32)],
        compiler_params=params(8),
        name="finish",
    )(own, back)


def step_z(a, d):
    return lax.ppermute(a, "ctx", [(i, (i + NY * d) % (NZ * NY)) for i in range(NZ * NY)])


def step_y(a, d):
    return lax.ppermute(
        a, "ctx", [(z * NY + y, z * NY + (y + d) % NY) for z in range(NZ) for y in range(NY)]
    )


def step_x(a, d):
    return lax.ppermute(a, "head", [(i, (i + 2 * d) % (2 * NX)) for i in range(2 * NX)])


def swap_core(a):
    return lax.ppermute(a, "head", [(i, i ^ 1) for i in range(2 * NX)])


def local(q_latent, q_rope, out_grad, kv_latent, key_rope, block_lists, query_pos):
    ctx = lax.axis_index("ctx")
    head = lax.axis_index("head")
    my_z, my_y = ctx // NY, ctx % NY
    me = jnp.stack([head, ctx * (OWN * 128)]).astype(jnp.int32)

    shard = pack_call(kv_latent, key_rope)
    columns = [[z * NY + y for z in range(NZ)] for y in range(NY)]
    shards = lax.all_to_all(shard, "ctx", 0, 0, tiled=True, axis_index_groups=columns)

    block_lists, me, query_pos = after((block_lists, me, query_pos), shard)
    every = jnp.arange(NZ * NY * OWN, dtype=jnp.int32)
    present = jnp.any(block_lists.reshape(-1)[:, None] == every[None, :], axis=0)
    remote = present & (every // OWN != ctx)
    grid = remote.reshape(NZ * NY, OWN)
    want = jnp.max(jnp.where(grid, jnp.arange(OWN, dtype=jnp.int32)[None, :], -1), axis=1)
    rank = jnp.cumsum(remote.astype(jnp.int32)) - 1
    slot_ids = jnp.arange(16, dtype=jnp.int32)
    match = remote[None, :] & (rank[None, :] == slot_ids[:, None])
    remote_ids = jnp.max(jnp.where(match, every[None, :], -1), axis=1)
    owner = jnp.maximum(remote_ids, 0) // OWN
    src = jnp.where(
        remote_ids >= 0, ((my_y - owner % NY) % NY) * NZ + (my_z - owner // NY) % NZ, 0
    ).astype(jnp.int32)
    ctxs = jnp.arange(SLOTS, dtype=jnp.int32)
    hit = (remote_ids[None, :] >= 0) & (remote_ids[None, :] // OWN == ctxs[:, None])
    back_at = jnp.sum(jnp.where(hit, slot_ids[None, :], 0), axis=1).astype(jnp.int32)
    wants = [want] + [step_y(want, -d) for d in range(1, NY)]
    chosen = jnp.any(block_lists[:, None, :] == remote_ids[None, :, None], axis=2)
    chosen = chosen & (remote_ids >= 0)[None, :]
    far_bias = jnp.where(chosen, 0.0, NEG_FILL).astype(F32).T

    cols = pick_y_call(wants, shards)
    cols = [cols[0]] + [step_y(cols[d], d) for d in range(1, NY)]
    x0 = pick_x_call(src, cols)
    x2, x1, x3 = step_x(x0, 2), step_x(x0, 1), step_x(x0, -1)
    xs = [x0, x1, x2, x3]
    arrays = after((kv_latent, key_rope, q_latent, q_rope, out_grad), x0)
    own_keys, q, g = prep_call(*arrays)
    own_s, own_top = own_scores_call(me, query_pos.reshape(1, -1), own_keys, q)

    parts = list(far_scores_call(far_bias, x0, swap_core(x0), q))
    xs[1:] = after(xs[1:], own_top, parts[2])
    for dx in LATE:
        parts += [xs[dx], swap_core(xs[dx])]
    keys, p, ds = scores_call(far_bias, own_keys, own_s, own_top, parts, q, g)

    order = (2, 1, 3, 0)
    keep, send, part, got = {}, {}, {}, {}
    for n, dx in enumerate(order):
        keep[dx], send[dx] = dkv_call(dx, p, ds, q, g)
        p, ds = after((p, ds), send[dx])
        if n:
            prev = order[n - 1]
            part[prev] = (keep[prev] + swap_core(send[prev]).astype(F32)).astype(BF)
            got[prev] = step_x(part[prev], -prev)
            p, ds = after((p, ds), part[prev])
    swap = swap_core(send[0])
    dq_latent, dq_rope = dq_call(ds, keys)
    mine, dq_latent, dq_rope = lax.optimization_barrier((keep[0], dq_latent, dq_rope))

    slots, own = slots_call(back_at, want, mine, swap, got[1], got[2], got[3])
    back = lax.all_to_all(slots, "ctx", split_axis=0, concat_axis=0, tiled=True)
    dkv_latent, dkey_rope = finish_call(own, back)
    return (dq_latent, dq_rope, dkv_latent, dkey_rope)


def solution(mesh):
    return jax.shard_map(
        local,
        mesh=mesh,
        in_specs=(
            P("ctx", "head"),
            P("ctx", "head"),
            P("ctx", "head"),
            P("ctx", None, None),
            P("ctx", None, None),
            P("ctx", None),
            P("ctx"),
        ),
        out_specs=(
            P("ctx", "head"),
            P("ctx", "head"),
            P("ctx", "head", None),
            P("ctx", "head", None),
        ),
        check_vma=False,
    )
```

```python
import functools

import jax
import jax.numpy as jnp
from jax import lax
from jax.experimental import pallas as pl
from jax.experimental.pallas import tpu as pltpu
from jax.sharding import PartitionSpec as P

SCALE_FACTOR = 192.0 ** (-0.5)
LOG2E = 1.4426950408889634
NEG_FILL = -1e30
BF = jnp.bfloat16
F32 = jnp.float32
LAT = 512
WIDE = 640
SHARE = 16
REMOTE = 13
OWN = 4
FAR_ROWS = REMOTE * SHARE
GROUP = (REMOTE + OWN) * SHARE
GROUPS = 8
KEYS = GROUP * GROUPS
CHIP = 2 * GROUP
HEADS = 8
ROWS = 1024
CH = 256
NCH = ROWS // CH
SPAN = OWN * SHARE
SLOTS = 32
TILES = LAT // 128
BLOCK_ROWS = TILES * SHARE
SHARD_ROWS = OWN * BLOCK_ROWS + OWN // 2 * SHARE
COL_LAT = 8 * BLOCK_ROWS
COL_ROWS = COL_LAT + 4 * SHARE
FAR_LAT = REMOTE * BLOCK_ROWS
FAR_PACKED = FAR_LAT + (REMOTE + 1) // 2 * SHARE
GRAD_LAT = (REMOTE + OWN) * BLOCK_ROWS
GRAD_ROWS = GRAD_LAT + (REMOTE + OWN + 1) // 2 * SHARE
NZ, NY, NX = 8, 4, 4


def params(mib):
    return pltpu.CompilerParams(vmem_limit_bytes=mib * 1024 * 1024)


def after(x, *deps):
    return lax.optimization_barrier((x,) + deps)[0]


def cost(flops, nbytes):
    return pl.CostEstimate(flops=flops, bytes_accessed=nbytes, transcendentals=0)


def vspec():
    return pl.BlockSpec(memory_space=pltpu.VMEM)


def hbm_spec():
    return pl.BlockSpec(memory_space=pltpu.HBM)


def nt_dot(a, b):
    return lax.dot_general(a, b, (((1,), (1,)), ((), ())), preferred_element_type=F32)


def tn_dot(a, b):
    return lax.dot_general(a, b, (((0,), (0,)), ((), ())), preferred_element_type=F32)


def left_lanes(wide):
    lane = lax.broadcasted_iota(jnp.int32, wide.shape, 1)
    return jnp.where(lane < 64, wide, 0.0)


def pair_tile(even, odd):
    lane = lax.broadcasted_iota(jnp.int32, even.shape, 1)
    return jnp.where(lane < 64, even, pltpu.roll(odd, 64, 1))


def half_tile(tile, odd):
    wide = tile.astype(F32)
    return jnp.where(odd == 1, pltpu.roll(wide, 64, 1), wide)


def unpack_rope(packed, core):
    row = lax.broadcasted_iota(jnp.int32, (SHARE, SHARE), 0)
    col = lax.broadcasted_iota(jnp.int32, (SHARE, SHARE), 1)
    pick = jnp.where(col == core * 8 + row // 2, 1.0, 0.0).astype(BF)
    wide = jnp.dot(pick, packed, preferred_element_type=F32)
    odd = lax.broadcasted_iota(jnp.int32, (SHARE, 128), 0) % 2 == 1
    return left_lanes(jnp.where(odd, pltpu.roll(wide, 64, 1), wide))


def pack_body(kv_ref, rope_ref, out_ref, lat, rope, sems):
    head = lax.axis_index("head")
    wide = kv_ref.at[:, pl.ds(pl.multiple_of(head * SHARE, SHARE), SHARE), :]
    thin = rope_ref.at[:, pl.ds(pl.multiple_of(head // 2 * SHARE, SHARE), SHARE), :]
    copies = (
        pltpu.make_async_copy(wide, lat, sems.at[0]),
        pltpu.make_async_copy(thin, rope, sems.at[1]),
    )
    for copy in copies:
        copy.start()
    for copy in copies:
        copy.wait()
    tiles = [lat[b, :, t * 128:(t + 1) * 128] for b in range(OWN) for t in range(TILES)]
    thin_rows = [unpack_rope(rope[b], head % 2) for b in range(OWN)]
    tiles += [pair_tile(*thin_rows[b:b + 2]).astype(BF) for b in range(0, OWN, 2)]
    for z in range(NZ):
        for n, tile in enumerate(tiles):
            at = z * SHARD_ROWS + n * SHARE
            out_ref[at:at + SHARE, :] = tile


def pack_call(kv, rope):
    return pl.pallas_call(
        pack_body,
        in_specs=[hbm_spec()] * 2,
        out_specs=vspec(),
        out_shape=jax.ShapeDtypeStruct((NZ * SHARD_ROWS, 128), BF),
        scratch_shapes=[
            pltpu.VMEM((OWN, SHARE, LAT), BF),
            pltpu.VMEM((OWN, SHARE, 128), BF),
            pltpu.SemaphoreType.DMA((2,)),
        ],
        compiler_params=params(56),
        name="pack_share",
    )(kv, rope)


def share_of(me, g):
    return (me // 2 + NX - g // 2) % NX, (me % 2 + g % 2) % 2


def prep_body(kv_hbm, rope_hbm, q_hbm, qr_hbm, g_hbm, own_out, q_out, g_out,
              kv_ref, rope_ref, qr_ref, sems):
    copies = [
        pltpu.make_async_copy(qr_hbm, qr_ref, sems.at[0]),
        pltpu.make_async_copy(rope_hbm, rope_ref, sems.at[1]),
        pltpu.make_async_copy(kv_hbm, kv_ref, sems.at[2]),
    ]
    for h in range(HEADS):
        cols, rows = pl.ds(h * LAT, LAT), pl.ds(h * 128, 128)
        copies.append(pltpu.make_async_copy(
            q_hbm.at[:, cols], q_out.at[rows, pl.ds(0, LAT)], sems.at[3 + 2 * h]))
        copies.append(pltpu.make_async_copy(
            g_hbm.at[:, cols], g_out.at[rows, :], sems.at[4 + 2 * h]))
    for copy in copies:
        copy.start()
    me = lax.axis_index("head")
    lane = lax.broadcasted_iota(jnp.int32, (128, 128), 1)
    copies[0].wait()
    for h in range(HEADS):
        pair = qr_ref[:, (h // 2) * 128:(h // 2 + 1) * 128].astype(F32)
        if h % 2:
            pair = pltpu.roll(pair, 64, 1)
        q_out[h * 128:(h + 1) * 128, LAT:] = jnp.where(lane < 64, pair, 0.0).astype(BF)
    copies[1].wait()
    for g in range(GROUPS):
        chip, core = share_of(me, g)
        for b in range(OWN):
            own_out[g, b * SHARE:(b + 1) * SHARE, LAT:] = unpack_rope(
                rope_ref[b, pl.ds(pl.multiple_of(chip * SHARE, SHARE), SHARE), :], core
            ).astype(BF)
    copies[2].wait()
    for g in range(GROUPS):
        chip, core = share_of(me, g)
        at = pl.multiple_of((chip * 2 + core) * SHARE, SHARE)
        for b in range(OWN):
            own_out[g, b * SHARE:(b + 1) * SHARE, :LAT] = kv_ref[b, pl.ds(at, SHARE), :]
    for copy in copies[3:]:
        copy.wait()


def prep_call(kv, rope, q, qr, g):
    return pl.pallas_call(
        prep_body,
        in_specs=[hbm_spec()] * 5,
        out_specs=[vspec()] * 3,
        out_shape=[
            jax.ShapeDtypeStruct((GROUPS, SPAN, WIDE), BF),
            jax.ShapeDtypeStruct((ROWS, WIDE), BF),
            jax.ShapeDtypeStruct((ROWS, LAT), BF),
        ],
        scratch_shapes=[
            pltpu.VMEM(kv.shape, BF),
            pltpu.VMEM(rope.shape, BF),
            pltpu.VMEM(qr.shape, BF),
            pltpu.SemaphoreType.DMA((3 + 2 * HEADS,)),
        ],
        compiler_params=params(10),
        cost_estimate=cost(1000, 10_000_000),
        name="prep_operands",
    )(kv, rope, q, qr, g)


def rows_at(ref, at, count):
    return ref[pl.ds(pl.multiple_of(at, SHARE), count), :]


def pick_y_body(*refs):
    wants, shards, outs = refs[:NY], refs[NY], refs[NY + 1:]
    ctx = lax.axis_index("ctx")
    for dy in range(NY):
        thin = []
        for r in range(NZ):
            z = (ctx // NY + NZ - r) % NZ
            w = jnp.maximum(wants[dy][z * NY + ctx % NY], 0)
            base = z * SHARD_ROWS
            outs[dy][r * BLOCK_ROWS:(r + 1) * BLOCK_ROWS, :] = rows_at(
                shards, base + w * BLOCK_ROWS, BLOCK_ROWS
            )
            tile = rows_at(shards, base + OWN * BLOCK_ROWS + w // 2 * SHARE, SHARE)
            thin.append(half_tile(tile, w % 2))
        for r in range(0, NZ, 2):
            at = COL_LAT + r // 2 * SHARE
            outs[dy][at:at + SHARE, :] = pair_tile(thin[r], thin[r + 1]).astype(BF)


def pick_y_call(wants, shards):
    return pl.pallas_call(
        pick_y_body,
        in_specs=[pl.BlockSpec(memory_space=pltpu.SMEM)] * NY + [vspec()],
        out_specs=[vspec()] * NY,
        out_shape=[jax.ShapeDtypeStruct((COL_ROWS, 128), BF)] * NY,
        compiler_params=params(4),
        name="pick_for_y_peers",
    )(*wants, shards)


def pick_x_body(src_ref, y0, y1, y2, y3, out_ref, stage):
    for dy, ref in enumerate((y0, y1, y2, y3)):
        stage[dy * COL_ROWS:(dy + 1) * COL_ROWS, :] = ref[...]
    thin = []
    for u in range(REMOTE):
        base, r = src_ref[u] // NZ * COL_ROWS, src_ref[u] % NZ
        out_ref[u * BLOCK_ROWS:(u + 1) * BLOCK_ROWS, :] = rows_at(
            stage, base + r * BLOCK_ROWS, BLOCK_ROWS
        )
        thin.append(half_tile(rows_at(stage, base + COL_LAT + r // 2 * SHARE, SHARE), r % 2))
    for u in range(0, REMOTE, 2):
        at = FAR_LAT + u // 2 * SHARE
        odd = thin[min(u + 1, REMOTE - 1)]
        out_ref[at:at + SHARE, :] = pair_tile(thin[u], odd).astype(BF)


def pick_x_call(src, cols):
    return pl.pallas_call(
        pick_x_body,
        in_specs=[pl.BlockSpec(memory_space=pltpu.SMEM)] + [vspec()] * NY,
        out_specs=vspec(),
        out_shape=jax.ShapeDtypeStruct((FAR_PACKED, 128), BF),
        scratch_shapes=[pltpu.VMEM((NY * COL_ROWS, 128), BF)],
        compiler_params=params(4),
        name="pick_selected",
    )(src, *cols)


def log_scores(keys, q, bias):
    s = nt_dot(keys, q) * (SCALE_FACTOR * LOG2E)
    return s + jnp.concatenate([bias, bias], axis=1)


def fill_far(refs, k_out, starts):
    for ref, start in zip(refs, starts):
        for u in range(REMOTE):
            rows = slice(start + u * SHARE, start + (u + 1) * SHARE)
            for t in range(TILES):
                at = u * BLOCK_ROWS + t * SHARE
                k_out[rows, t * 128:(t + 1) * 128] = ref[at:at + SHARE, :]
            at = FAR_LAT + u // 2 * SHARE
            k_out[rows, LAT:] = left_lanes(half_tile(ref[at:at + SHARE, :], u % 2)).astype(BF)


def fill_far_bias(far_ref, bias_scr):
    for u in range(REMOTE):
        bias_scr[u * SHARE:(u + 1) * SHARE, :] = jnp.broadcast_to(
            far_ref[u:u + 1, :], (SHARE, 128)
        )


def far_scores_body(far_ref, x_ref, c_ref, q_ref, k_out, s_out, top_out, bias_scr):
    fill_far((x_ref, c_ref), k_out, (0, FAR_ROWS))
    fill_far_bias(far_ref, bias_scr)
    for c in range(NCH):
        q = q_ref[c * CH:(c + 1) * CH, :]
        top = jnp.full((1, CH), -jnp.inf, F32)
        for cr in range(2):
            rows = slice(cr * FAR_ROWS, (cr + 1) * FAR_ROWS)
            s = log_scores(k_out[rows, :], q, bias_scr[...])
            s_out[c, rows, :] = s
            top = jnp.maximum(top, jnp.max(s, axis=0, keepdims=True))
        top_out[c] = top


def far_scores_call(far, x, c, q):
    return pl.pallas_call(
        far_scores_body,
        in_specs=[vspec()] * 4,
        out_specs=[vspec()] * 3,
        out_shape=[
            jax.ShapeDtypeStruct((2 * FAR_ROWS, WIDE), BF),
            jax.ShapeDtypeStruct((NCH, 2 * FAR_ROWS, CH), F32),
            jax.ShapeDtypeStruct((NCH, 1, CH), F32),
        ],
        scratch_shapes=[pltpu.VMEM((FAR_ROWS, 128), F32)],
        compiler_params=params(10),
        cost_estimate=cost(2 * 2 * FAR_ROWS * ROWS * 640, 4_000_000),
        name="far_scores",
    )(far, x, c, q)


def own_scores_body(me_ref, pos_ref, own_ref, q_ref, s_out, top_out, bias_scr):
    pos = pos_ref[...] - me_ref[1]
    step = lax.broadcasted_iota(jnp.int32, (SHARE, 128), 0)
    for g in range(GROUPS):
        chip, core = share_of(me_ref[0], g)
        for b in range(OWN):
            at = g * SPAN + b * SHARE
            key = step + (b * 128 + (chip * 2 + core) * SHARE)
            bias_scr[at:at + SHARE, :] = jnp.where(key <= pos, 0.0, NEG_FILL)
    for c in range(NCH):
        q = q_ref[c * CH:(c + 1) * CH, :]
        top = jnp.full((1, CH), -jnp.inf, F32)
        for n in range(2):
            rows = slice(n * 4 * SPAN, (n + 1) * 4 * SPAN)
            keys = own_ref[4 * n:4 * n + 4].reshape(4 * SPAN, WIDE)
            s = log_scores(keys, q, bias_scr[rows, :])
            s_out[c, rows, :] = s
            top = jnp.maximum(top, jnp.max(s, axis=0, keepdims=True))
        top_out[c] = top


def own_scores_call(me, pos, own, q):
    return pl.pallas_call(
        own_scores_body,
        in_specs=[pl.BlockSpec(memory_space=pltpu.SMEM)] + [vspec()] * 3,
        out_specs=[vspec()] * 2,
        out_shape=[
            jax.ShapeDtypeStruct((NCH, GROUPS * SPAN, CH), F32),
            jax.ShapeDtypeStruct((NCH, 1, CH), F32),
        ],
        scratch_shapes=[pltpu.VMEM((GROUPS * SPAN, 128), F32)],
        compiler_params=params(10),
        cost_estimate=cost(2 * GROUPS * SPAN * ROWS * 640, 4_000_000),
        name="own_scores",
    )(me, pos, own, q)


EARLY = (0,)
LATE = tuple(dx for dx in range(NX) if dx not in EARLY)


def scores_body(far_ref, own, own_s, own_top, *refs):
    done = {dx: refs[3 * n:3 * n + 3] for n, dx in enumerate(EARLY)}
    refs = refs[3 * len(EARLY):]
    late = {dx: refs[2 * n:2 * n + 2] for n, dx in enumerate(LATE)}
    q_ref, g_ref, k_out, p_out, ds_out, s_scr, e_scr, bias_scr = refs[2 * len(LATE):]
    fill_far_bias(far_ref, bias_scr)
    for g in range(GROUPS):
        at, dx, cr = g * GROUP, g // 2, g % 2
        if dx in done:
            k_out[at:at + FAR_ROWS, :] = done[dx][0][cr * FAR_ROWS:(cr + 1) * FAR_ROWS, :]
        else:
            fill_far(late[dx][cr:cr + 1], k_out, (at,))
        k_out[at + FAR_ROWS:at + GROUP, :] = own[g]

    for c in range(NCH):
        q = q_ref[c * CH:(c + 1) * CH, :]
        grad = g_ref[c * CH:(c + 1) * CH, :]
        top = own_top[c]
        for dx in EARLY:
            top = jnp.maximum(top, done[dx][2][c])
        for dx in LATE:
            for g in (2 * dx, 2 * dx + 1):
                rows = slice(g * GROUP, g * GROUP + FAR_ROWS)
                s = log_scores(k_out[rows, :], q, bias_scr[...])
                s_scr[rows, :] = s
                top = jnp.maximum(top, jnp.max(s, axis=0, keepdims=True))
        total = jnp.zeros((1, CH), F32)
        delta = jnp.zeros((1, CH), F32)
        for g in range(GROUPS):
            at, dx, cr = g * GROUP, g // 2, g % 2
            rows = slice(at, at + GROUP)
            e = nt_dot(k_out[rows, :LAT], grad)
            e_scr[rows, :] = e
            if dx in done:
                far = done[dx][1][c, cr * FAR_ROWS:(cr + 1) * FAR_ROWS, :]
            else:
                far = s_scr[at:at + FAR_ROWS, :]
            s = jnp.concatenate([far, own_s[c, g * SPAN:(g + 1) * SPAN, :]], axis=0)
            w = jnp.exp2(s - top)
            s_scr[rows, :] = w
            total = total + jnp.sum(w, axis=0, keepdims=True)
            delta = delta + jnp.sum(w * e, axis=0, keepdims=True)
        inv = 1.0 / total
        delta = delta * inv
        for g in range(GROUPS):
            rows = slice(g * GROUP, (g + 1) * GROUP)
            p = s_scr[rows, :] * inv
            p_out[c, rows, :] = p.astype(BF)
            ds_out[c, rows, :] = ((e_scr[rows, :] - delta) * (p * SCALE_FACTOR)).astype(BF)


def scores_call(far, own, own_s, own_top, parts, q, g):
    return pl.pallas_call(
        scores_body,
        in_specs=[vspec()] * (4 + len(parts) + 2),
        out_specs=[vspec()] * 3,
        out_shape=[
            jax.ShapeDtypeStruct((KEYS, WIDE), BF),
            jax.ShapeDtypeStruct((NCH, KEYS, CH), BF),
            jax.ShapeDtypeStruct((NCH, KEYS, CH), BF),
        ],
        scratch_shapes=[
            pltpu.VMEM((KEYS, CH), F32),
            pltpu.VMEM((KEYS, CH), F32),
            pltpu.VMEM((FAR_ROWS, 128), F32),
        ],
        compiler_params=params(30),
        cost_estimate=cost(2 * KEYS * ROWS * 1152, 16_000_000),
        name="scores",
    )(far, own, own_s, own_top, *parts, q, g)


def dkv_body(p_ref, ds_ref, q_ref, g_ref, keep_ref, send_ref):
    for cr, out in enumerate((keep_ref, send_ref)):
        rows = slice(cr * GROUP, (cr + 1) * GROUP)
        ds = jnp.concatenate([ds_ref[c, rows, :] for c in range(NCH)], axis=1)
        p = jnp.concatenate([p_ref[c, rows, :] for c in range(NCH)], axis=1)
        a = jnp.dot(ds, q_ref[...], preferred_element_type=F32)
        b = jnp.dot(p, g_ref[...], preferred_element_type=F32)
        lat, thin = a[:, :LAT] + b, a[:, LAT:]
        for u in range(REMOTE + OWN):
            mine = slice(u * SHARE, (u + 1) * SHARE)
            for t in range(TILES):
                at = u * BLOCK_ROWS + t * SHARE
                out[at:at + SHARE, :] = lat[mine, t * 128:(t + 1) * 128].astype(out.dtype)
        for u in range(0, REMOTE + OWN, 2):
            at = GRAD_LAT + u // 2 * SHARE
            odd = min(u + 1, REMOTE + OWN - 1)
            pair = pair_tile(thin[u * SHARE:(u + 1) * SHARE], thin[odd * SHARE:(odd + 1) * SHARE])
            out[at:at + SHARE, :] = pair.astype(out.dtype)


def dkv_call(dx, p, ds, q, g):
    part = pl.BlockSpec((NCH, CHIP, CH), lambda i: (0, dx, 0))
    return pl.pallas_call(
        dkv_body,
        grid=(1,),
        in_specs=[part, part, pl.BlockSpec((ROWS, WIDE), lambda i: (0, 0)),
                  pl.BlockSpec((ROWS, LAT), lambda i: (0, 0))],
        out_specs=[pl.BlockSpec((GRAD_ROWS, 128), lambda i: (0, 0))] * 2,
        out_shape=[
            jax.ShapeDtypeStruct((GRAD_ROWS, 128), F32),
            jax.ShapeDtypeStruct((GRAD_ROWS, 128), BF),
        ],
        compiler_params=params(16),
        cost_estimate=cost(2 * CHIP * ROWS * 1152, 5_000_000),
        name=f"dkv_chunk{dx}",
    )(p, ds, q, g)


def dq_body(ds_ref, k_ref, lat_ref, rope_ref):
    res = tn_dot(ds_ref[0], k_ref[...])
    lat_ref[:, :LAT] = res[:128, :LAT].astype(BF)
    lat_ref[:, LAT:] = res[128:, :LAT].astype(BF)
    lane = lax.broadcasted_iota(jnp.int32, (128, 128), 1)
    odd = pltpu.roll(res[128:, LAT:], 64, 1)
    rope_ref[...] = jnp.where(lane < 64, res[:128, LAT:], odd).astype(BF)


def dq_call(ds, keys):
    return pl.pallas_call(
        dq_body,
        grid=(NCH,),
        in_specs=[
            pl.BlockSpec((1, KEYS, CH), lambda i: (i, 0, 0)),
            pl.BlockSpec((KEYS, WIDE), lambda i: (0, 0)),
        ],
        out_specs=[
            pl.BlockSpec((128, 2 * LAT), lambda i: (0, i)),
            pl.BlockSpec((128, 128), lambda i: (0, i)),
        ],
        out_shape=[
            jax.ShapeDtypeStruct((128, HEADS * LAT), BF),
            jax.ShapeDtypeStruct((128, HEADS * 64), BF),
        ],
        compiler_params=params(14),
        cost_estimate=cost(2 * KEYS * ROWS * 640, 8_000_000),
        name="dq",
    )(ds, keys)


def slots_body(at_ref, want_ref, keep_ref, swap_ref, r1_ref, r2_ref, r3_ref,
               slot_out, own_out, far):
    total = keep_ref[...] + swap_ref[...].astype(F32)
    for ref in (r1_ref, r2_ref, r3_ref):
        total = total + ref[...].astype(F32)
    far[...] = total
    for b in range(OWN):
        u, rows = REMOTE + b, slice(b * SHARE, (b + 1) * SHARE)
        for t in range(TILES):
            at = u * BLOCK_ROWS + t * SHARE
            own_out[rows, t * 128:(t + 1) * 128] = far[at:at + SHARE, :]
        at = GRAD_LAT + u // 2 * SHARE
        own_out[rows, LAT:] = left_lanes(half_tile(far[at:at + SHARE, :], u % 2))
    lane = lax.broadcasted_iota(jnp.int32, (SHARE, 128), 1)
    for c in range(SLOTS):
        rows = slice(c * SHARE, (c + 1) * SHARE)
        w = want_ref[c]
        flag = jnp.where(w >= 0, 64 + w, 128)
        u = at_ref[c]
        for t in range(TILES):
            tile = rows_at(far, u * BLOCK_ROWS + t * SHARE, SHARE)
            slot_out[rows, t * 128:(t + 1) * 128] = tile.astype(BF)
        thin = left_lanes(half_tile(rows_at(far, GRAD_LAT + u // 2 * SHARE, SHARE), u % 2))
        slot_out[rows, LAT:] = jnp.where(lane == flag, 1.0, thin).astype(BF)


def slots_call(at, want, keep, swap, r1, r2, r3):
    smem = pl.BlockSpec(memory_space=pltpu.SMEM)
    return pl.pallas_call(
        slots_body,
        in_specs=[smem, smem] + [vspec()] * 5,
        out_specs=[vspec()] * 2,
        out_shape=[
            jax.ShapeDtypeStruct((SLOTS * SHARE, WIDE), BF),
            jax.ShapeDtypeStruct((SPAN, WIDE), F32),
        ],
        scratch_shapes=[pltpu.VMEM((GRAD_ROWS, 128), F32)],
        compiler_params=params(8),
        name="fill_slots",
    )(at, want, keep, swap, r1, r2, r3)


def finish_body(own_ref, back_ref, lat_ref, rope_ref, acc, scr):
    acc[...] = own_ref[...]
    for c in range(SLOTS):
        piece = back_ref[c * SHARE:(c + 1) * SHARE, :].astype(F32)
        for b in range(OWN):
            mine = piece[:, LAT + 64 + b:LAT + 65 + b] > 0.5
            acc[b * SHARE:(b + 1) * SHARE, :] += jnp.where(mine, piece, 0.0)
    for b in range(OWN):
        lat_ref[b] = acc[b * SHARE:(b + 1) * SHARE, :LAT]
    scr[...] = acc[:, LAT:]
    half = SPAN // 2
    even = scr[pl.ds(0, half, 2), :]
    odd = scr[pl.ds(1, half, 2), :]
    lane = lax.broadcasted_iota(jnp.int32, (half, 128), 1)
    both = jnp.where(lane < 64, even, pltpu.roll(odd, 64, 1))
    rope_ref[...] = both.reshape(OWN, SHARE // 2, 128)


def finish_call(own, back):
    return pl.pallas_call(
        finish_body,
        in_specs=[vspec()] * 2,
        out_specs=[vspec()] * 2,
        out_shape=[
            jax.ShapeDtypeStruct((OWN, SHARE, LAT), F32),
            jax.ShapeDtypeStruct((OWN, SHARE // 2, 128), F32),
        ],
        scratch_shapes=[pltpu.VMEM((SPAN, WIDE), F32), pltpu.VMEM((SPAN, 128), F32)],
        compiler_params=params(8),
        name="finish",
    )(own, back)


def step_z(a, d):
    return lax.ppermute(a, "ctx", [(i, (i + NY * d) % (NZ * NY)) for i in range(NZ * NY)])


def step_y(a, d):
    return lax.ppermute(
        a, "ctx", [(z * NY + y, z * NY + (y + d) % NY) for z in range(NZ) for y in range(NY)]
    )


def step_x(a, d):
    return lax.ppermute(a, "head", [(i, (i + 2 * d) % (2 * NX)) for i in range(2 * NX)])


def swap_core(a):
    return lax.ppermute(a, "head", [(i, i ^ 1) for i in range(2 * NX)])


def local(q_latent, q_rope, out_grad, kv_latent, key_rope, block_lists, query_pos):
    ctx = lax.axis_index("ctx")
    head = lax.axis_index("head")
    my_z, my_y = ctx // NY, ctx % NY
    me = jnp.stack([head, ctx * (OWN * 128)]).astype(jnp.int32)

    shard = pack_call(kv_latent, key_rope)
    columns = [[z * NY + y for z in range(NZ)] for y in range(NY)]
    shards = lax.all_to_all(shard, "ctx", 0, 0, tiled=True, axis_index_groups=columns)

    block_lists, me, query_pos = after((block_lists, me, query_pos), shard)
    every = jnp.arange(NZ * NY * OWN, dtype=jnp.int32)
    present = jnp.any(block_lists.reshape(-1)[:, None] == every[None, :], axis=0)
    remote = present & (every // OWN != ctx)
    grid = remote.reshape(NZ * NY, OWN)
    want = jnp.max(jnp.where(grid, jnp.arange(OWN, dtype=jnp.int32)[None, :], -1), axis=1)
    rank = jnp.cumsum(remote.astype(jnp.int32)) - 1
    slot_ids = jnp.arange(16, dtype=jnp.int32)
    match = remote[None, :] & (rank[None, :] == slot_ids[:, None])
    remote_ids = jnp.max(jnp.where(match, every[None, :], -1), axis=1)
    owner = jnp.maximum(remote_ids, 0) // OWN
    src = jnp.where(
        remote_ids >= 0, ((my_y - owner % NY) % NY) * NZ + (my_z - owner // NY) % NZ, 0
    ).astype(jnp.int32)
    ctxs = jnp.arange(SLOTS, dtype=jnp.int32)
    hit = (remote_ids[None, :] >= 0) & (remote_ids[None, :] // OWN == ctxs[:, None])
    back_at = jnp.sum(jnp.where(hit, slot_ids[None, :], 0), axis=1).astype(jnp.int32)
    wants = [want] + [step_y(want, -d) for d in range(1, NY)]
    chosen = jnp.any(block_lists[:, None, :] == remote_ids[None, :, None], axis=2)
    chosen = chosen & (remote_ids >= 0)[None, :]
    far_bias = jnp.where(chosen, 0.0, NEG_FILL).astype(F32).T

    cols = pick_y_call(wants, shards)
    cols = [cols[0]] + [step_y(cols[d], d) for d in range(1, NY)]
    x0 = pick_x_call(src, cols)
    x2, x1, x3 = step_x(x0, 2), step_x(x0, 1), step_x(x0, -1)
    xs = [x0, x1, x2, x3]
    arrays = after((kv_latent, key_rope, q_latent, q_rope, out_grad), x0)
    own_keys, q, g = prep_call(*arrays)
    own_s, own_top = own_scores_call(me, query_pos.reshape(1, -1), own_keys, q)

    parts = list(far_scores_call(far_bias, x0, swap_core(x0), q))
    x2, x3 = after((xs[2], xs[3]), own_top, parts[2])
    c2, c3 = swap_core(x2), swap_core(x3)
    x1 = after(xs[1], own_top, parts[2], c2, c3)
    parts += [x1, swap_core(x1), x2, c2, x3, c3]
    keys, p, ds = scores_call(far_bias, own_keys, own_s, own_top, parts, q, g)

    order = (2, 1, 3, 0)
    keep, send, part, got = {}, {}, {}, {}
    for n, dx in enumerate(order):
        keep[dx], send[dx] = dkv_call(dx, p, ds, q, g)
        p, ds = after((p, ds), send[dx])
        if n:
            prev = order[n - 1]
            part[prev] = (keep[prev] + swap_core(send[prev]).astype(F32)).astype(BF)
            got[prev] = step_x(part[prev], -prev)
            p, ds = after((p, ds), part[prev])
    swap = swap_core(send[0])
    dq_latent, dq_rope = dq_call(ds, keys)
    mine, dq_latent, dq_rope = lax.optimization_barrier((keep[0], dq_latent, dq_rope))

    slots, own = slots_call(back_at, want, mine, swap, got[1], got[2], got[3])
    back = lax.all_to_all(slots, "ctx", split_axis=0, concat_axis=0, tiled=True)
    dkv_latent, dkey_rope = finish_call(own, back)
    return (dq_latent, dq_rope, dkv_latent, dkey_rope)


def solution(mesh):
    return jax.shard_map(
        local,
        mesh=mesh,
        in_specs=(
            P("ctx", "head"),
            P("ctx", "head"),
            P("ctx", "head"),
            P("ctx", None, None),
            P("ctx", None, None),
            P("ctx", None),
            P("ctx"),
        ),
        out_specs=(
            P("ctx", "head"),
            P("ctx", "head"),
            P("ctx", "head", None),
            P("ctx", "head", None),
        ),
        check_vma=False,
    )
```
